256 devices in a mesh: row: 16 (over y, x_hi, core), col: 16 (over z, x_lo).
Axes of the slice: x: 4 (x_hi: 2, x_lo: 2; x = x_hi * 2 + x_lo), y: 4, z: 8, core: 2. Of those that a mesh axis runs over, the one named last changes fastest.
Arguments:
- pair: bfloat16 [512, 512, 128], P('row', 'col'), may hold values from -1.5 to 1.5
- norm_gain: float32 [3, 128], replicated, may hold values from 0.1 to 1.9
- norm_bias: float32 [3, 128], replicated, may hold values from -3 to 3
- proj_weight: bfloat16 [2, 128, 640], replicated, may hold values from -0.5 to 0.5
- out_gain: float32 [2, 128], replicated, may hold values from 0.1 to 1.9
- out_bias: float32 [2, 128], replicated, may hold values from -3 to 3
- out_weight: bfloat16 [2, 128, 128], replicated, may hold values from -1 to 1
- up_weight: bfloat16 [128, 1024], replicated, may hold values from -0.5 to 0.5
- down_weight: bfloat16 [512, 128], replicated, may hold values from -0.25 to 0.25
Outputs:
- updated: bfloat16 [512, 512, 128], P('row', 'col')
The draws below stay inside these ranges and needn't reach their ends.
All inputs are finite; a program needn't handle non-finite values.
Results may differ from the reference program's by a relative error of at most 0.029.
Values may be sent and summed in bfloat16 or wider, within the bound.
No kernel may reach another device: no remote copies, remote signals or barrier semaphores. Data moves between devices by JAX's collectives and lax.ppermute only.
A program may use at most 128 MiB of HBM per device.

```python
import jax
import jax.numpy as jnp
from jax import lax

C = 128
HID = 128
FF = 512
N_RES = 512


def draw_pair(key, part):
    key = jax.random.fold_in(key, 11)
    first = jax.random.fold_in(key, 0)
    values = 0.25 * jax.random.normal(first, (N_RES, N_RES, C), jnp.float32)
    return jnp.clip(values, -1.5, 1.5).astype(jnp.bfloat16)


def draw_norm_bias(key, part):
    key = jax.random.fold_in(key, 12)
    values = jnp.clip(jax.random.normal(key, (3, C), jnp.float32), -2.5, 2.5)
    factor = jnp.where(jnp.arange(3)[:, None] < 2, 0.02, 0.5).astype(jnp.float32)
    return values * factor


def draw_out_bias(key, part):
    key = jax.random.fold_in(key, 13)
    values = jnp.clip(jax.random.normal(key, (2, HID), jnp.float32), -2.5, 2.5)
    factor = jnp.where(jnp.arange(2)[:, None] < 1, 0.02, 0.5).astype(jnp.float32)
    return values * factor


def bell_draw(rng, extent, deviation, reach, dtype=jnp.bfloat16):
    values = jax.random.normal(rng, extent, jnp.float32) * deviation
    return jnp.minimum(jnp.maximum(values, -reach), reach).astype(dtype)


def setup_inputs(seed: int = 0) -> dict:
    arg_keys = jax.random.split(jax.random.key(seed), 10)
    pair = draw_pair(jax.random.fold_in(arg_keys[9], 71), 0)
    norm_gain = jnp.clip(1.0 + 0.18 * jax.random.normal(arg_keys[1], (3, C), jnp.float32), 0.1, 1.9)
    norm_bias = draw_norm_bias(jax.random.fold_in(arg_keys[9], 71), 0)
    proj_weight = bell_draw(arg_keys[3], (2, C, 4 * HID + C), C ** -0.5, 0.5)
    out_gain = jnp.clip(1.0 + 0.18 * jax.random.normal(arg_keys[4], (2, HID), jnp.float32), 0.1, 1.9)
    out_bias = draw_out_bias(jax.random.fold_in(arg_keys[9], 71), 0)
    out_weight = bell_draw(arg_keys[6], (2, HID, C), (HID // 4) ** -0.5, 1.0)
    up_weight = bell_draw(arg_keys[7], (C, 2 * FF), C ** -0.5, 0.5)
    down_weight = bell_draw(arg_keys[8], (FF, C), FF ** -0.5, 0.25)
    return {"pair": pair, "norm_gain": norm_gain, "norm_bias": norm_bias, "proj_weight": proj_weight, "out_gain": out_gain, "out_bias": out_bias, "out_weight": out_weight, "up_weight": up_weight, "down_weight": down_weight}


def layer_norm(values, gain, bias):
    mean = lax.optimization_barrier(jnp.mean(values, axis=-1, keepdims=True))
    centred = values - mean
    var = lax.optimization_barrier(jnp.mean(centred * centred, axis=-1, keepdims=True))
    return centred * jax.lax.rsqrt(var + 1e-05) * gain + bias

def triangle(field, which, norm_gain, norm_bias, proj_weight, out_gain, out_bias, out_weight, incoming):
    hidden = out_weight.shape[1]
    size = field.shape[0]
    width = field.shape[2]
    normed = layer_norm(field, norm_gain[which], norm_bias[which]).astype(jnp.bfloat16)
    proj = jnp.dot(normed.reshape(size * size, width), proj_weight[which], preferred_element_type=jnp.float32)
    proj = proj.reshape(size, size, -1)
    left = (jax.nn.sigmoid(proj[..., :hidden]) * proj[..., hidden:2 * hidden]).astype(jnp.bfloat16)
    right = (jax.nn.sigmoid(proj[..., 2 * hidden:3 * hidden]) * proj[..., 3 * hidden:4 * hidden]).astype(jnp.bfloat16)
    gate = jax.nn.sigmoid(proj[..., 4 * hidden:])
    if incoming:
        mixed = jnp.einsum('kic,kjc->ijc', left.astype(jnp.float32), right.astype(jnp.float32))
    else:
        mixed = jnp.einsum('ikc,jkc->ijc', left.astype(jnp.float32), right.astype(jnp.float32))
    mixnorm = layer_norm(mixed, out_gain[which], out_bias[which]).astype(jnp.bfloat16)
    branch = jnp.dot(mixnorm.reshape(size * size, hidden), out_weight[which], preferred_element_type=jnp.float32)
    return field + gate * branch.reshape(size, size, width)

def reference(pair, norm_gain, norm_bias, proj_weight, out_gain, out_bias, out_weight, up_weight, down_weight):
    size = pair.shape[0]
    width = pair.shape[2]
    inner = down_weight.shape[0]
    field = pair.astype(jnp.float32)
    field = triangle(field, 0, norm_gain, norm_bias, proj_weight, out_gain, out_bias, out_weight, False)
    field = triangle(field, 1, norm_gain, norm_bias, proj_weight, out_gain, out_bias, out_weight, True)
    tnorm = layer_norm(field, norm_gain[2], norm_bias[2]).astype(jnp.bfloat16)
    expanded = jnp.dot(tnorm.reshape(size * size, width), up_weight, preferred_element_type=jnp.float32)
    act = (jax.nn.silu(expanded[:, :inner]) * expanded[:, inner:]).astype(jnp.bfloat16)
    back = jnp.dot(act, down_weight, preferred_element_type=jnp.float32).reshape(size, size, width)
    return (field + back).astype(jnp.bfloat16)
```

```python
import jax
import jax.numpy as jnp
from jax import lax
from jax.experimental import pallas as pl
from jax.experimental.pallas import tpu as pltpu
from jax.sharding import PartitionSpec as P

F32 = jnp.float32
BF16 = jnp.bfloat16
WIDTH = 128
SIDE = 32
STEPS = 8
FOLD = 4
PAIRS = 8
COLS = 16
CHUNK = 2

PARITY = [[(2 * a + core) * COLS + q for a in range(PAIRS) for q in range(COLS)] for core in (0, 1)]


def exchange(values):
    return lax.all_to_all(values, ("row", "col"), 0, 0, axis_index_groups=PARITY)


def swap_cores(values):
    return lax.ppermute(values, "row", [(i, i ^ 1) for i in range(2 * PAIRS)])


def column(ref, which):
    return jnp.broadcast_to(ref[which : which + 1, :], (WIDTH, WIDTH)).T[:, :1]


def layer_norm(values, gain, bias):
    mean = jnp.mean(values, axis=0, keepdims=True)
    centred = values - mean
    var = jnp.mean(centred * centred, axis=0, keepdims=True)
    return centred * lax.rsqrt(var + 1e-05) * gain + bias


def dot(a, b):
    return lax.dot_general(a, b, (((1,), (0,)), ((), ())), preferred_element_type=F32)


def prepare(field, gain, bias, weight):
    normed = layer_norm(field, gain, bias).astype(BF16)
    proj = dot(weight, normed)
    h = WIDTH
    left = jax.nn.sigmoid(proj[:h]) * proj[h : 2 * h]
    right = jax.nn.sigmoid(proj[2 * h : 3 * h]) * proj[3 * h : 4 * h]
    gate = jax.nn.sigmoid(proj[4 * h :])
    return left, right, gate


def finish(field, mixed, gain, bias, weight, gate):
    mixnorm = layer_norm(mixed, gain, bias).astype(BF16)
    return field + gate * dot(weight, mixnorm)


def put_factors(scratch, chunk, left, right):
    for i in range(CHUNK):
        step = chunk * CHUNK + i
        lanes = slice(i * 128, (i + 1) * 128)
        scratch[pl.ds(step, WIDTH, stride=2 * STEPS), :] = left[:, lanes]
        scratch[pl.ds(step + STEPS, WIDTH, stride=2 * STEPS), :] = right[:, lanes]


def take_mixed(scratch, chunk):
    parts = [
        scratch[pl.ds(chunk * CHUNK + i, WIDTH, stride=STEPS), :] for i in range(CHUNK)
    ]
    return jnp.concatenate(parts, axis=1)


def lanes_of(chunk):
    return slice(chunk * CHUNK * 128, (chunk + 1) * CHUNK * 128)


def first_kernel(pair, norm_gain, norm_bias, weight, factors, gates, fields, scratch):
    gain, bias = column(norm_gain, 0), column(norm_bias, 0)
    weight = weight[0].T
    for chunk in range(STEPS // CHUNK):
        parts = []
        for i in range(CHUNK):
            block = pair[:, chunk * CHUNK + i].astype(F32)
            parts.append(block.reshape(FOLD * SIDE, WIDTH).T)
        field = jnp.concatenate(parts, axis=1)
        left, right, gate = prepare(field, gain, bias, weight)
        put_factors(scratch, chunk, left, right)
        gates[:, lanes_of(chunk)] = gate
        fields[:, lanes_of(chunk)] = field
    factors[...] = scratch[...].reshape(WIDTH, 2 * STEPS, 128).astype(BF16)


def middle_kernel(
    mixed, gates, fields, norm_gain, norm_bias, weight, out_gain, out_bias, out_weight,
    factors, gates_out, fields_out, scratch, product,
):
    gain, bias = column(norm_gain, 1), column(norm_bias, 1)
    mix_gain, mix_bias = column(out_gain, 0), column(out_bias, 0)
    weight = weight[1].T
    out_w = out_weight[0].T
    product[...] = mixed[...].astype(F32).reshape(WIDTH * STEPS, 128)
    for chunk in range(STEPS // CHUNK):
        lanes = lanes_of(chunk)
        field = finish(
            fields[:, lanes], take_mixed(product, chunk), mix_gain, mix_bias, out_w, gates[:, lanes]
        )
        left, right, gate = prepare(field, gain, bias, weight)
        put_factors(scratch, chunk, left, right)
        gates_out[:, lanes] = gate
        fields_out[:, lanes] = field
    factors[...] = scratch[...].reshape(WIDTH, 2 * STEPS, 128).astype(BF16)


def last_kernel(
    mixed, gates, fields, norm_gain, norm_bias, out_gain, out_bias, out_weight, up, down,
    updated, product,
):
    gain, bias = column(norm_gain, 2), column(norm_bias, 2)
    mix_gain, mix_bias = column(out_gain, 1), column(out_bias, 1)
    out_w = out_weight[1].T
    up_w = up[...].T
    down_w = down[...].T
    inner = down.shape[0]
    product[...] = mixed[...].astype(F32).reshape(WIDTH * STEPS, 128)
    for chunk in range(STEPS // CHUNK):
        lanes = lanes_of(chunk)
        field = finish(
            fields[:, lanes], take_mixed(product, chunk), mix_gain, mix_bias, out_w, gates[:, lanes]
        )
        tnorm = layer_norm(field, gain, bias).astype(BF16)
        expanded = dot(up_w, tnorm)
        act = (jax.nn.silu(expanded[:inner]) * expanded[inner:]).astype(BF16)
        field = field + dot(down_w, act)
        for i in range(CHUNK):
            block = field[:, i * 128 : (i + 1) * 128].T.reshape(FOLD, SIDE, WIDTH)
            updated[:, chunk * CHUNK + i] = block.astype(BF16)


def turn(tiles):
    lane = lax.broadcasted_iota(jnp.int32, tiles[0].shape, 1)
    low = lane < 64
    even = (lane & 32) == 0
    a, b, c, d = tiles
    a, c = jnp.where(low, a, pltpu.roll(c, 64, 1)), jnp.where(low, pltpu.roll(a, 64, 1), c)
    b, d = jnp.where(low, b, pltpu.roll(d, 64, 1)), jnp.where(low, pltpu.roll(b, 64, 1), d)
    a, b = jnp.where(even, a, pltpu.roll(b, 32, 1)), jnp.where(even, pltpu.roll(a, 96, 1), b)
    c, d = jnp.where(even, c, pltpu.roll(d, 32, 1)), jnp.where(even, pltpu.roll(c, 96, 1), d)
    return a, b, c, d


def rows_of(tiles):
    return jnp.concatenate(turn(tiles), axis=0).astype(BF16)


def send_product(mixed, product):
    for a in range(PAIRS):
        for g in range(COLS // FOLD):
            tiles = [
                mixed[a * SIDE + i * STEPS : a * SIDE + (i + 1) * STEPS, g * 128 : (g + 1) * 128]
                for i in range(FOLD)
            ]
            for i, tile in enumerate(turn(tiles)):
                product[a * COLS + g * FOLD + i] = tile.astype(BF16)


def outgoing_kernel(own, other, product, left, right):
    core = lax.rem(lax.axis_index("row"), 2)

    def form(a, _):
        for g in range(COLS // FOLD):
            lanes = slice(g * 128, (g + 1) * 128)
            mine = [own[a * COLS + g * FOLD + i].astype(F32) for i in range(FOLD)]
            left[pl.ds(a * SIDE, SIDE), lanes] = rows_of([t[:STEPS] for t in mine])
            row = pl.multiple_of((2 * a + core) * SIDE, SIDE)
            right[pl.ds(row, SIDE), lanes] = rows_of([t[STEPS:] for t in mine])
            theirs = [other[a * COLS + g * FOLD + i].astype(F32) for i in range(FOLD)]
            row = pl.multiple_of((2 * a + 1 - core) * SIDE, SIDE)
            right[pl.ds(row, SIDE), lanes] = rows_of([t[STEPS:] for t in theirs])
        return 0

    lax.fori_loop(0, PAIRS, form, 0)
    mixed = lax.dot_general(
        left[...], right[...], (((1,), (1,)), ((), ())), preferred_element_type=F32
    )
    send_product(mixed, product)


def incoming_kernel(own, other, product, left, right):
    core = lax.rem(lax.axis_index("row"), 2)

    def form(a, _):
        for part, source in enumerate((own, other)):
            row = pl.ds(part * PAIRS * SIDE + a * SIDE, SIDE)
            for g in range(COLS // FOLD):
                tiles = [source[a * COLS + g * FOLD + i].astype(F32) for i in range(FOLD)]
                right[row, g * 128 : (g + 1) * 128] = rows_of([t[STEPS:] for t in tiles])
            for g in range(COLS // FOLD // 2):
                tiles = [
                    source[a * COLS + 2 * (g * FOLD + i) + core].astype(F32) for i in range(FOLD)
                ]
                left[row, g * 128 : (g + 1) * 128] = rows_of([t[:STEPS] for t in tiles])
        return 0

    lax.fori_loop(0, PAIRS, form, 0)
    mixed = lax.dot_general(
        left[...], right[...], (((0,), (0,)), ((), ())), preferred_element_type=F32
    )
    send_product(mixed, product)


def call(kernel, outs, scratch, name):
    return pl.pallas_call(
        kernel,
        out_shape=outs,
        scratch_shapes=scratch,
        compiler_params=pltpu.CompilerParams(vmem_limit_bytes=40 * 1024 * 1024),
        name=name,
    )


def multiply(kernel, factors, shapes, name):
    other = swap_cores(factors)
    product = jax.ShapeDtypeStruct((WIDTH, STEPS, 128), BF16)
    scratch = [pltpu.VMEM(shape, BF16) for shape in shapes]
    return call(kernel, product, scratch, name)(factors, other)


def body(
    pair, norm_gain, norm_bias, proj_weight, out_gain, out_bias, out_weight, up_weight, down_weight
):
    flat = jax.ShapeDtypeStruct((WIDTH, STEPS * 128), F32)
    packed = jax.ShapeDtypeStruct((WIDTH, 2 * STEPS, 128), BF16)
    packing = pltpu.VMEM((WIDTH * 2 * STEPS, 128), F32)
    unpacking = pltpu.VMEM((WIDTH * STEPS, 128), F32)
    size = PAIRS * SIDE

    factors, gate, field = call(first_kernel, (packed, flat, flat), [packing], "first")(
        pair.reshape(FOLD, STEPS, SIDE, WIDTH), norm_gain, norm_bias, proj_weight
    )
    factors = exchange(factors)
    shapes = ((size, 2 * size), (2 * size, 2 * size))
    mixed = exchange(multiply(outgoing_kernel, factors, shapes, "outgoing"))
    factors, gate, field = call(
        middle_kernel, (packed, flat, flat), [packing, unpacking], "middle"
    )(mixed, gate, field, norm_gain, norm_bias, proj_weight, out_gain, out_bias, out_weight)
    factors = exchange(factors)
    shapes = ((2 * size, size), (2 * size, 2 * size))
    mixed = exchange(multiply(incoming_kernel, factors, shapes, "incoming"))
    out = jax.ShapeDtypeStruct((FOLD, STEPS, SIDE, WIDTH), BF16)
    updated = call(last_kernel, out, [unpacking], "last")(
        mixed, gate, field, norm_gain, norm_bias, out_gain, out_bias, out_weight,
        up_weight, down_weight,
    )
    return updated.reshape(FOLD * STEPS, SIDE, WIDTH)


def solution(mesh):
    placed = (P("row", "col", None), P(), P(), P(), P(), P(), P(), P(), P())
    return jax.shard_map(
        body, mesh=mesh, in_specs=placed, out_specs=P("row", "col", None), check_vma=False
    )
```

```python
import jax
import jax.numpy as jnp
from jax import lax
from jax.experimental import pallas as pl
from jax.experimental.pallas import tpu as pltpu
from jax.sharding import PartitionSpec as P

F32 = jnp.float32
BF16 = jnp.bfloat16
WIDTH = 128
SIDE = 32
STEPS = 8
FOLD = 4
PAIRS = 8
COLS = 16
HALF = PAIRS * SIDE
FULL = 2 * HALF
CHUNK = 8

PARITY = [[(2 * a + core) * COLS + q for q in range(COLS) for a in range(PAIRS)] for core in (0, 1)]


def member(a, q):
    return q * PAIRS + a


def exchange(values):
    return lax.all_to_all(values, ("row", "col"), 0, 0, axis_index_groups=PARITY)


def swap_cores(values):
    return lax.ppermute(values, "row", [(i, i ^ 1) for i in range(2 * PAIRS)])


def core_index():
    return lax.rem(lax.axis_index("row"), 2)


def sigmoid(x):
    return 0.5 + 0.5 * jnp.tanh(0.5 * x)


def layer_norm(values, gain, bias):
    mean = jnp.mean(values, axis=0, keepdims=True)
    centred = values - mean
    var = jnp.mean(centred * centred, axis=0, keepdims=True)
    return centred * lax.rsqrt(var + 1e-05) * gain + bias


def dot(a, b):
    return lax.dot_general(a, b, (((1,), (0,)), ((), ())), preferred_element_type=F32)


def prepare(field, gain, bias, weight):
    normed = layer_norm(field, gain, bias).astype(BF16)
    proj = dot(weight, normed)
    h = WIDTH
    left = sigmoid(proj[:h]) * proj[h : 2 * h]
    right = sigmoid(proj[2 * h : 3 * h]) * proj[3 * h : 4 * h]
    gate = sigmoid(proj[4 * h :])
    return left, right, gate


def finish(field, mixed, gain, bias, weight, gate):
    mixnorm = layer_norm(mixed, gain, bias).astype(BF16)
    return field + gate * dot(weight, mixnorm)


def put_factors(scratch, chunk, left, right):
    for i in range(CHUNK):
        step = chunk * CHUNK + i
        lanes = slice(i * 128, (i + 1) * 128)
        scratch[pl.ds(step, WIDTH, stride=2 * STEPS), :] = left[:, lanes]
        scratch[pl.ds(step + STEPS, WIDTH, stride=2 * STEPS), :] = right[:, lanes]


def take_mixed(scratch, chunk):
    parts = [scratch[pl.ds(chunk * CHUNK + i, WIDTH, stride=STEPS), :] for i in range(CHUNK)]
    return jnp.concatenate(parts, axis=1)


def lanes_of(chunk):
    return slice(chunk * CHUNK * 128, (chunk + 1) * CHUNK * 128)


def first_kernel(
    pair_hbm, norm_gain_hbm, norm_bias_hbm, out_gain_hbm, out_bias_hbm, weight_hbm,
    factors, gates, fields, vectors,
    pair, norm_gain, norm_bias, out_gain, out_bias, weight, scratch, sems,
):
    copies = [
        pltpu.make_async_copy(source, target, sems.at[i])
        for i, (source, target) in enumerate(
            (
                (weight_hbm.at[0], weight),
                (pair_hbm, pair),
                (norm_gain_hbm, norm_gain),
                (norm_bias_hbm, norm_bias),
                (out_gain_hbm, out_gain),
                (out_bias_hbm, out_bias),
            )
        )
    ]
    for copy in copies:
        copy.start()
    for copy in copies:
        copy.wait()
    rows = [norm_gain[...], norm_bias[...], out_gain[...], out_bias[...]]
    rows = jnp.concatenate(rows + [jnp.zeros((WIDTH - 10, WIDTH), F32)], axis=0)
    vectors[...] = rows.T
    gain, bias = vectors[:, 0:1], vectors[:, 3:4]
    weight = weight[...].T
    for chunk in range(STEPS // CHUNK):
        parts = []
        for i in range(CHUNK):
            block = pair[:, chunk * CHUNK + i].astype(F32)
            parts.append(block.reshape(FOLD * SIDE, WIDTH).T)
        field = jnp.concatenate(parts, axis=1)
        left, right, gate = prepare(field, gain, bias, weight)
        put_factors(scratch, chunk, left, right)
        gates[:, lanes_of(chunk)] = gate
        fields[:, lanes_of(chunk)] = field
    factors[...] = scratch[...].reshape(WIDTH, 2 * STEPS, 128).astype(BF16)


def middle_kernel(
    mixed, gates, fields, vectors, weight, out_weight, factors, gates_out, fields_out,
    scratch, product,
):
    gain, bias = vectors[:, 1:2], vectors[:, 4:5]
    mix_gain, mix_bias = vectors[:, 6:7], vectors[:, 8:9]
    proj_w, out_w = weight[1].T, out_weight[0].T
    product[...] = mixed[...].astype(F32).reshape(WIDTH * STEPS, 128)
    for chunk in range(STEPS // CHUNK):
        lanes = lanes_of(chunk)
        field = finish(
            fields[:, lanes], take_mixed(product, chunk), mix_gain, mix_bias,
            out_w, gates[:, lanes],
        )
        left, right, gate = prepare(field, gain, bias, proj_w)
        put_factors(scratch, chunk, left, right)
        gates_out[:, lanes] = gate
        fields_out[:, lanes] = field
    factors[...] = scratch[...].reshape(WIDTH, 2 * STEPS, 128).astype(BF16)


def last_kernel(
    mixed, gates, fields, vectors, out_weight, up, down, updated, product
):
    gain, bias = vectors[:, 2:3], vectors[:, 5:6]
    mix_gain, mix_bias = vectors[:, 7:8], vectors[:, 9:10]
    out_w, up_w, down_w = out_weight[1].T, up[...].T, down[...].T
    inner = down.shape[0]
    product[...] = mixed[...].astype(F32).reshape(WIDTH * STEPS, 128)
    for chunk in range(STEPS // CHUNK):
        lanes = lanes_of(chunk)
        field = finish(
            fields[:, lanes], take_mixed(product, chunk), mix_gain, mix_bias,
            out_w, gates[:, lanes],
        )
        tnorm = layer_norm(field, gain, bias).astype(BF16)
        expanded = dot(up_w, tnorm)
        wide = expanded[:inner]
        act = (wide * sigmoid(wide) * expanded[inner:]).astype(BF16)
        field = field + dot(down_w, act)
        for i in range(CHUNK):
            block = field[:, i * 128 : (i + 1) * 128].T.reshape(FOLD, SIDE, WIDTH)
            updated[:, chunk * CHUNK + i] = block.astype(BF16)


def turn(tiles):
    lane = lax.broadcasted_iota(jnp.int32, tiles[0].shape, 1)
    low = lane < 64
    even = (lane & 32) == 0
    a, b, c, d = tiles
    a, c = jnp.where(low, a, pltpu.roll(c, 64, 1)), jnp.where(low, pltpu.roll(a, 64, 1), c)
    b, d = jnp.where(low, b, pltpu.roll(d, 64, 1)), jnp.where(low, pltpu.roll(b, 64, 1), d)
    a, b = jnp.where(even, a, pltpu.roll(b, 32, 1)), jnp.where(even, pltpu.roll(a, 96, 1), b)
    c, d = jnp.where(even, c, pltpu.roll(d, 32, 1)), jnp.where(even, pltpu.roll(c, 96, 1), d)
    return a, b, c, d


def rows_of(tiles):
    return jnp.concatenate(turn(tiles), axis=0).astype(BF16)


def left_of(source, a, q):
    return source[member(a, q), :STEPS].astype(F32)


def right_of(source, a, q):
    return source[member(a, q), STEPS:].astype(F32)


def lanes_from(g):
    return slice(g * 128, (g + 1) * 128)


def send_product(mixed, product):
    for a in range(PAIRS):
        rows = [slice(a * SIDE + i * STEPS, a * SIDE + (i + 1) * STEPS) for i in range(FOLD)]
        for g in range(COLS // FOLD):
            for i, tile in enumerate(turn([mixed[row, lanes_from(g)] for row in rows])):
                product[member(a, g * FOLD + i)] = tile.astype(BF16)


def outgoing_kernel(own, other, product, left, right):
    core = core_index()

    def form(a, _):
        mine = pl.ds(pl.multiple_of((2 * a + core) * SIDE, SIDE), SIDE)
        theirs = pl.ds(pl.multiple_of((2 * a + 1 - core) * SIDE, SIDE), SIDE)
        for g in range(COLS // FOLD):
            columns = [g * FOLD + i for i in range(FOLD)]
            left[pl.ds(a * SIDE, SIDE), lanes_from(g)] = rows_of(
                [left_of(own, a, q) for q in columns]
            )
            right[mine, lanes_from(g)] = rows_of([right_of(own, a, q) for q in columns])
            right[theirs, lanes_from(g)] = rows_of([right_of(other, a, q) for q in columns])
        return 0

    lax.fori_loop(0, PAIRS, form, 0)
    mixed = lax.dot_general(
        left[...], right[...], (((1,), (1,)), ((), ())), preferred_element_type=F32
    )
    send_product(mixed, product)


def incoming_kernel(own, other, product, left, right):
    core = core_index()

    def form(a, _):
        for part, source in enumerate((own, other)):
            row = pl.ds(part * HALF + a * SIDE, SIDE)
            for g in range(COLS // FOLD):
                columns = [g * FOLD + i for i in range(FOLD)]
                right[row, lanes_from(g)] = rows_of([right_of(source, a, q) for q in columns])
            for g in range(PAIRS // FOLD):
                columns = [2 * (g * FOLD + i) + core for i in range(FOLD)]
                left[row, lanes_from(g)] = rows_of([left_of(source, a, q) for q in columns])
        return 0

    lax.fori_loop(0, PAIRS, form, 0)
    mixed = lax.dot_general(
        left[...], right[...], (((0,), (0,)), ((), ())), preferred_element_type=F32
    )
    send_product(mixed, product)


def call(kernel, outs, scratch, name, vmem=40, **more):
    return pl.pallas_call(
        kernel,
        out_shape=outs,
        scratch_shapes=scratch,
        compiler_params=pltpu.CompilerParams(vmem_limit_bytes=vmem * 1024 * 1024),
        name=name,
        **more,
    )


def shape(*dims, dtype=BF16):
    return jax.ShapeDtypeStruct(dims, dtype)


def body(
    pair, norm_gain, norm_bias, proj_weight, out_gain, out_bias, out_weight, up_weight, down_weight
):
    flat = shape(WIDTH, STEPS * 128, dtype=F32)
    packed = shape(WIDTH, 2 * STEPS, 128)
    product = shape(WIDTH, STEPS, 128)
    packing = pltpu.VMEM((WIDTH * 2 * STEPS, 128), F32)
    unpacking = pltpu.VMEM((WIDTH * STEPS, 128), F32)
    blocks = (FOLD, STEPS, SIDE, WIDTH)

    operands = (pair.reshape(blocks), norm_gain, norm_bias, out_gain, out_bias)
    landing = [pltpu.VMEM(v.shape, v.dtype) for v in operands]
    landing += [pltpu.VMEM(proj_weight.shape[1:], BF16), packing, pltpu.SemaphoreType.DMA((6,))]
    factors, gate, field, vectors = call(
        first_kernel, (packed, flat, flat, shape(WIDTH, WIDTH, dtype=F32)), landing, "first", 60,
        in_specs=[pl.BlockSpec(memory_space=pltpu.HBM)] * 6,
    )(*operands, proj_weight)
    own = exchange(factors)
    left, right = pltpu.VMEM((HALF, FULL), BF16), pltpu.VMEM((FULL, FULL), BF16)
    mixed = call(outgoing_kernel, product, [left, right], "outgoing")(own, swap_cores(own))
    factors, gate, field = call(
        middle_kernel, (packed, flat, flat), [packing, unpacking], "middle"
    )(exchange(mixed), gate, field, vectors, proj_weight, out_weight)
    own = exchange(factors)
    left = pltpu.VMEM((FULL, HALF), BF16)
    mixed = call(incoming_kernel, product, [left, right], "incoming")(own, swap_cores(own))
    updated = call(last_kernel, shape(*blocks), [unpacking], "last")(
        exchange(mixed), gate, field, vectors, out_weight, up_weight, down_weight
    )
    return updated.reshape(FOLD * STEPS, SIDE, WIDTH)


def solution(mesh):
    placed = (P("row", "col", None), P(), P(), P(), P(), P(), P(), P(), P())
    return jax.shard_map(
        body, mesh=mesh, in_specs=placed, out_specs=P("row", "col", None), check_vma=False
    )
```

```python
import jax
import jax.numpy as jnp
from jax import lax
from jax.experimental import pallas as pl
from jax.experimental.pallas import tpu as pltpu
from jax.sharding import PartitionSpec as P

F32 = jnp.float32
BF16 = jnp.bfloat16
WIDTH = 128
SIDE = 32
STEPS = 8
FOLD = 4
PAIRS = 8
COLS = 16
HALF = PAIRS * SIDE
FULL = 2 * HALF

PARITY = [[(2 * a + core) * COLS + q for q in range(COLS) for a in range(PAIRS)] for core in (0, 1)]


def member(a, q):
    return q * PAIRS + a


def exchange(values):
    return lax.all_to_all(values, ("row", "col"), 0, 0, axis_index_groups=PARITY)


def swap_cores(values):
    return lax.ppermute(values, "row", [(i, i ^ 1) for i in range(2 * PAIRS)])


def core_index():
    return lax.rem(lax.axis_index("row"), 2)


def sigmoid(x):
    return 0.5 + 0.5 * jnp.tanh(0.5 * x)


def layer_norm(values, gain, bias):
    mean = jnp.mean(values, axis=0, keepdims=True)
    centred = values - mean
    var = jnp.mean(centred * centred, axis=0, keepdims=True)
    return centred * lax.rsqrt(var + 1e-05) * gain + bias


def dot(a, b):
    return lax.dot_general(a, b, (((1,), (0,)), ((), ())), preferred_element_type=F32)


def finish(field, mixed, gain, bias, weight, gate):
    mixnorm = layer_norm(mixed, gain, bias).astype(BF16)
    return field + gate * dot(weight, mixnorm)


def take_mixed(mixed, scratch):
    scratch[...] = mixed[...].astype(F32).reshape(WIDTH * STEPS, 128)
    steps = [scratch[pl.ds(step, WIDTH, stride=STEPS), :] for step in range(STEPS)]
    return jnp.concatenate(steps, axis=1)


def field_of(pair):
    rows = pair[...].astype(F32)
    steps = [rows[:, i].reshape(FOLD * SIDE, WIDTH).T for i in range(STEPS)]
    return jnp.concatenate(steps, axis=1)


def columns_of(refs):
    rows = jnp.concatenate([ref[...] for ref in refs], axis=0)
    rest = jnp.zeros((WIDTH - rows.shape[0], WIDTH), F32)
    return jnp.concatenate([rows, rest], axis=0).T


def factors_of(proj):
    h = WIDTH
    left = sigmoid(proj[:h]) * proj[h : 2 * h]
    right = sigmoid(proj[2 * h : 3 * h]) * proj[3 * h : 4 * h]
    return left, right


def put_factors(scratch, left, right, factors):
    for step in range(STEPS):
        lanes = slice(step * 128, (step + 1) * 128)
        scratch[pl.ds(step, WIDTH, stride=2 * STEPS), :] = left[:, lanes]
        scratch[pl.ds(step + STEPS, WIDTH, stride=2 * STEPS), :] = right[:, lanes]
    factors[...] = scratch[...].reshape(WIDTH, 2 * STEPS, 128).astype(BF16)


def first_kernel(
    pair_hbm, gain_hbm, bias_hbm, weight_hbm, factors, pair, gain, bias, weight, scratch, sems
):
    sources = (weight_hbm.at[0], pair_hbm, gain_hbm, bias_hbm)
    targets = (weight, pair, gain, bias)
    copies = [
        pltpu.make_async_copy(source, target, sems.at[i])
        for i, (source, target) in enumerate(zip(sources, targets))
    ]
    for copy in copies:
        copy.start()
    for copy in copies:
        copy.wait()
    vectors = columns_of((gain, bias))
    normed = layer_norm(field_of(pair), vectors[:, 0:1], vectors[:, 3:4]).astype(BF16)
    left, right = factors_of(dot(weight[:, : 4 * WIDTH].T, normed))
    put_factors(scratch, left, right, factors)


def gate_kernel(
    pair, norm_gain, norm_bias, out_gain, out_bias, weight, _, gates, fields, vectors
):
    vectors[...] = columns_of((norm_gain, norm_bias, out_gain, out_bias))
    field = field_of(pair)
    normed = layer_norm(field, vectors[:, 0:1], vectors[:, 3:4]).astype(BF16)
    gates[...] = sigmoid(dot(weight[0, :, 4 * WIDTH :].T, normed))
    fields[...] = field


def middle_kernel(
    mixed, gates, fields, vectors, weight, out_weight, factors, fields_out, scratch, product
):
    gain, bias = vectors[:, 1:2], vectors[:, 4:5]
    mix_gain, mix_bias = vectors[:, 6:7], vectors[:, 8:9]
    field = finish(
        fields[...], take_mixed(mixed, product), mix_gain, mix_bias, out_weight[0].T, gates[...]
    )
    normed = layer_norm(field, gain, bias).astype(BF16)
    put_factors(scratch, *factors_of(dot(weight[1, :, : 4 * WIDTH].T, normed)), factors)
    fields_out[...] = field


def second_gate_kernel(fields, vectors, weight, _, gates):
    normed = layer_norm(fields[...], vectors[:, 1:2], vectors[:, 4:5]).astype(BF16)
    gates[...] = sigmoid(dot(weight[1, :, 4 * WIDTH :].T, normed))


def last_kernel(mixed, gates, fields, vectors, out_weight, up, down, updated, product):
    gain, bias = vectors[:, 2:3], vectors[:, 5:6]
    mix_gain, mix_bias = vectors[:, 7:8], vectors[:, 9:10]
    inner = down.shape[0]
    field = finish(
        fields[...], take_mixed(mixed, product), mix_gain, mix_bias, out_weight[1].T, gates[...]
    )
    expanded = dot(up[...].T, layer_norm(field, gain, bias).astype(BF16))
    wide = expanded[:inner]
    act = (wide * sigmoid(wide) * expanded[inner:]).astype(BF16)
    field = field + dot(down[...].T, act)
    for i in range(STEPS):
        block = field[:, i * 128 : (i + 1) * 128].T.reshape(FOLD, SIDE, WIDTH)
        updated[:, i] = block.astype(BF16)


def turn(tiles):
    lane = lax.broadcasted_iota(jnp.int32, tiles[0].shape, 1)
    low = lane < 64
    even = (lane & 32) == 0

    def far(a, b):
        moved = pltpu.roll(jnp.where(low, b, a), 64, 1)
        return jnp.where(low, a, moved), jnp.where(low, moved, b)

    def near(a, b):
        return (
            jnp.where(even, a, pltpu.roll(b, 32, 1)),
            jnp.where(even, pltpu.roll(a, 96, 1), b),
        )

    a, b, c, d = tiles
    a, c = far(a, c)
    b, d = far(b, d)
    return *near(a, b), *near(c, d)


def lanes_from(g):
    return slice(g * 128, (g + 1) * 128)


def rows_of(source, columns, half):
    rows = slice(half * STEPS, (half + 1) * STEPS)
    tiles = [
        source[pl.ds(member(0, q), PAIRS), rows, :].astype(F32).reshape(PAIRS * STEPS, 128)
        for q in columns
    ]
    tiles = [tile.reshape(PAIRS, 1, STEPS, 128) for tile in turn(tiles)]
    return jnp.concatenate(tiles, axis=1)


def flat_rows(block):
    return block.reshape(HALF, 128).astype(BF16)


def send_product(mixed, product):
    mixed = mixed.reshape(PAIRS, FOLD, STEPS, FULL)
    for g in range(COLS // FOLD):
        tiles = [mixed[:, i, :, lanes_from(g)].reshape(PAIRS * STEPS, 128) for i in range(FOLD)]
        for i, tile in enumerate(turn(tiles)):
            rows = pl.ds(member(0, g * FOLD + i), PAIRS)
            product[rows] = tile.reshape(PAIRS, STEPS, 128).astype(BF16)


def outgoing_kernel(own, other, _, product, left, right):
    core = core_index()
    for g in range(COLS // FOLD):
        columns = [g * FOLD + i for i in range(FOLD)]
        left[:, lanes_from(g)] = flat_rows(rows_of(own, columns, 0))
        for source, parity in ((own, core), (other, 1 - core)):
            block = rows_of(source, columns, 1).reshape(PAIRS, SIDE, 128).astype(BF16)
            right[:, parity, :, lanes_from(g)] = block
    mixed = lax.dot_general(
        left[...], right[...].reshape(FULL, FULL), (((1,), (1,)), ((), ())),
        preferred_element_type=F32,
    )
    send_product(mixed, product)


def incoming_kernel(own, other, _, product, left, right):
    core = core_index()
    for part, source in enumerate((own, other)):
        rows = slice(part * HALF, (part + 1) * HALF)
        for g in range(COLS // FOLD):
            columns = [g * FOLD + i for i in range(FOLD)]
            right[rows, lanes_from(g)] = flat_rows(rows_of(source, columns, 1))
        for g in range(PAIRS // FOLD):
            columns = [2 * (g * FOLD + i) + core for i in range(FOLD)]
            left[rows, lanes_from(g)] = flat_rows(rows_of(source, columns, 0))
    mixed = lax.dot_general(
        left[...], right[...], (((0,), (0,)), ((), ())), preferred_element_type=F32
    )
    send_product(mixed, product)


def call(kernel, outs, scratch, name, vmem=40, **more):
    return pl.pallas_call(
        kernel,
        out_shape=outs,
        scratch_shapes=scratch,
        compiler_params=pltpu.CompilerParams(vmem_limit_bytes=vmem * 1024 * 1024),
        name=name,
        **more,
    )


def shape(*dims, dtype=BF16):
    return jax.ShapeDtypeStruct(dims, dtype)


def body(
    pair, norm_gain, norm_bias, proj_weight, out_gain, out_bias, out_weight, up_weight, down_weight
):
    flat = shape(WIDTH, STEPS * 128, dtype=F32)
    packed = shape(WIDTH, 2 * STEPS, 128)
    product = shape(WIDTH, STEPS, 128)
    packing = pltpu.VMEM((WIDTH * 2 * STEPS, 128), F32)
    unpacking = pltpu.VMEM((WIDTH * STEPS, 128), F32)
    blocks = (FOLD, STEPS, SIDE, WIDTH)

    pair = pair.reshape(blocks)
    operands = (pair, norm_gain, norm_bias)
    landing = [pltpu.VMEM(v.shape, v.dtype) for v in operands]
    landing += [pltpu.VMEM(proj_weight.shape[1:], BF16), packing, pltpu.SemaphoreType.DMA((4,))]
    hbm = pl.BlockSpec(memory_space=pltpu.HBM)
    vmem = pl.BlockSpec(memory_space=pltpu.VMEM)
    after = pl.BlockSpec(memory_space=pl.ANY)
    factors = call(first_kernel, packed, landing, "first", 60, in_specs=[hbm] * 4)(
        *operands, proj_weight
    )
    own = exchange(factors)
    other = swap_cores(own)
    gate, field, vectors = call(
        gate_kernel, (flat, flat, shape(WIDTH, WIDTH, dtype=F32)), [], "gate",
        in_specs=[vmem] * 6 + [after],
    )(pair, norm_gain, norm_bias, out_gain, out_bias, proj_weight, own)
    left, right = pltpu.VMEM((HALF, FULL), BF16), pltpu.VMEM((PAIRS, 2, SIDE, FULL), BF16)
    mixed = call(
        outgoing_kernel, product, [left, right], "outgoing", in_specs=[vmem, vmem, after]
    )(own, other, vectors)
    factors, field = call(middle_kernel, (packed, flat), [packing, unpacking], "middle")(
        exchange(mixed), gate, field, vectors, proj_weight, out_weight
    )
    own = exchange(factors)
    other = swap_cores(own)
    gate = call(second_gate_kernel, flat, [], "second_gate", in_specs=[vmem] * 3 + [after])(
        field, vectors, proj_weight, own
    )
    left, right = pltpu.VMEM((FULL, HALF), BF16), pltpu.VMEM((FULL, FULL), BF16)
    mixed = call(
        incoming_kernel, product, [left, right], "incoming", in_specs=[vmem, vmem, after]
    )(own, other, gate)
    updated = call(last_kernel, shape(*blocks), [unpacking], "last")(
        exchange(mixed), gate, field, vectors, out_weight, up_weight, down_weight
    )
    return updated.reshape(FOLD * STEPS, SIDE, WIDTH)


def solution(mesh):
    placed = (P("row", "col", None), P(), P(), P(), P(), P(), P(), P(), P())
    return jax.shard_map(
        body, mesh=mesh, in_specs=placed, out_specs=P("row", "col", None), check_vma=False
    )
```

```python
import jax
import jax.numpy as jnp
from jax import lax
from jax.experimental import pallas as pl
from jax.experimental.pallas import tpu as pltpu
from jax.sharding import PartitionSpec as P

F32 = jnp.float32
BF16 = jnp.bfloat16
WIDTH = 128
SIDE = 32
STEPS = 8
FOLD = 4
PAIRS = 8
COLS = 16
HALF = PAIRS * SIDE
FULL = 2 * HALF

PARITY = [[(2 * a + core) * COLS + q for q in range(COLS) for a in range(PAIRS)] for core in (0, 1)]


def member(a, q):
    return q * PAIRS + a


def exchange(values):
    return lax.all_to_all(values, ("row", "col"), 0, 0, axis_index_groups=PARITY)


def swap_cores(values):
    return lax.ppermute(values, "row", [(i, i ^ 1) for i in range(2 * PAIRS)])


def core_index():
    return lax.rem(lax.axis_index("row"), 2)


def sigmoid(x):
    return 0.5 + 0.5 * jnp.tanh(0.5 * x)


def layer_norm(values, gain, bias):
    mean = jnp.mean(values, axis=0, keepdims=True)
    centred = values - mean
    var = jnp.mean(centred * centred, axis=0, keepdims=True)
    return centred * lax.rsqrt(var + 1e-05) * gain + bias


def dot(a, b):
    return lax.dot_general(a, b, (((1,), (0,)), ((), ())), preferred_element_type=F32)


def finish(field, mixed, gain, bias, weight, gate):
    mixnorm = layer_norm(mixed, gain, bias).astype(BF16)
    return field + gate * dot(weight, mixnorm)


def take_mixed(mixed, scratch):
    scratch[...] = mixed[...].astype(F32).reshape(WIDTH * STEPS, 128)
    steps = [scratch[pl.ds(step, WIDTH, stride=STEPS), :] for step in range(STEPS)]
    return jnp.concatenate(steps, axis=1)


def field_of(pair):
    rows = pair[...].astype(F32)
    steps = [rows[:, i].reshape(FOLD * SIDE, WIDTH).T for i in range(STEPS)]
    return jnp.concatenate(steps, axis=1)


def columns_of(refs):
    rows = jnp.concatenate([ref[...] for ref in refs], axis=0)
    rest = jnp.zeros((WIDTH - rows.shape[0], WIDTH), F32)
    return jnp.concatenate([rows, rest], axis=0).T


def factors_of(proj):
    h = WIDTH
    left = sigmoid(proj[:h]) * proj[h : 2 * h]
    right = sigmoid(proj[2 * h : 3 * h]) * proj[3 * h : 4 * h]
    return left, right


def put_factors(scratch, left, right, factors):
    for step in range(STEPS):
        lanes = slice(step * 128, (step + 1) * 128)
        scratch[pl.ds(step, WIDTH, stride=2 * STEPS), :] = left[:, lanes]
        scratch[pl.ds(step + STEPS, WIDTH, stride=2 * STEPS), :] = right[:, lanes]
    factors[...] = scratch[...].reshape(WIDTH, 2 * STEPS, 128).astype(BF16)


def first_kernel(
    pair_hbm, gain_hbm, bias_hbm, weight_hbm, factors, pair, gain, bias, weight, scratch, sems
):
    sources = (weight_hbm.at[0], pair_hbm, gain_hbm, bias_hbm)
    targets = (weight, pair, gain, bias)
    copies = [
        pltpu.make_async_copy(source, target, sems.at[i])
        for i, (source, target) in enumerate(zip(sources, targets))
    ]
    for copy in copies:
        copy.start()
    for copy in copies:
        copy.wait()
    vectors = columns_of((gain, bias))
    normed = layer_norm(field_of(pair), vectors[:, 0:1], vectors[:, 3:4]).astype(BF16)
    left, right = factors_of(dot(weight[:, : 4 * WIDTH].T, normed))
    put_factors(scratch, left, right, factors)


def middle_kernel(
    mixed, gates, fields, vectors, weight, out_weight, factors, fields_out, scratch, product
):
    gain, bias = vectors[:, 1:2], vectors[:, 4:5]
    mix_gain, mix_bias = vectors[:, 6:7], vectors[:, 8:9]
    field = finish(
        fields[...], take_mixed(mixed, product), mix_gain, mix_bias, out_weight[0].T, gates[...]
    )
    normed = layer_norm(field, gain, bias).astype(BF16)
    put_factors(scratch, *factors_of(dot(weight[1, :, : 4 * WIDTH].T, normed)), factors)
    fields_out[...] = field


def last_kernel(mixed, gates, fields, vectors, out_weight, up, down, updated, product):
    gain, bias = vectors[:, 2:3], vectors[:, 5:6]
    mix_gain, mix_bias = vectors[:, 7:8], vectors[:, 9:10]
    inner = down.shape[0]
    field = finish(
        fields[...], take_mixed(mixed, product), mix_gain, mix_bias, out_weight[1].T, gates[...]
    )
    expanded = dot(up[...].T, layer_norm(field, gain, bias).astype(BF16))
    wide = expanded[:inner]
    act = (wide * sigmoid(wide) * expanded[inner:]).astype(BF16)
    field = field + dot(down[...].T, act)
    for i in range(STEPS):
        block = field[:, i * 128 : (i + 1) * 128].T.reshape(FOLD, SIDE, WIDTH)
        updated[:, i] = block.astype(BF16)


def turn(tiles):
    lane = lax.broadcasted_iota(jnp.int32, tiles[0].shape, 1)
    low = lane < 64
    even = (lane & 32) == 0

    def far(a, b):
        moved = pltpu.roll(jnp.where(low, b, a), 64, 1)
        return jnp.where(low, a, moved), jnp.where(low, moved, b)

    def near(a, b):
        return (
            jnp.where(even, a, pltpu.roll(b, 32, 1)),
            jnp.where(even, pltpu.roll(a, 96, 1), b),
        )

    a, b, c, d = tiles
    a, c = far(a, c)
    b, d = far(b, d)
    return *near(a, b), *near(c, d)


def lanes_from(g):
    return slice(g * 128, (g + 1) * 128)


def rows_of(source, columns, half):
    rows = slice(half * STEPS, (half + 1) * STEPS)
    tiles = [
        source[pl.ds(member(0, q), PAIRS), rows, :].astype(F32).reshape(PAIRS * STEPS, 128)
        for q in columns
    ]
    tiles = [tile.reshape(PAIRS, 1, STEPS, 128) for tile in turn(tiles)]
    return jnp.concatenate(tiles, axis=1)


def flat_rows(block):
    return block.reshape(HALF, 128).astype(BF16)


def send_product(mixed, product, columns):
    mixed = mixed.reshape(PAIRS, FOLD, STEPS, SIDE * len(columns))
    for g in range(len(columns) // FOLD):
        tiles = [mixed[:, i, :, lanes_from(g)].reshape(PAIRS * STEPS, 128) for i in range(FOLD)]
        for i, tile in enumerate(turn(tiles)):
            rows = pl.ds(member(0, columns[g * FOLD + i]), PAIRS)
            product[rows] = tile.reshape(PAIRS, STEPS, 128).astype(BF16)


def outgoing_own_kernel(
    own, pair, norm_gain, norm_bias, out_gain, out_bias, weight,
    left, right, gates, fields, vectors,
):
    for g in range(COLS // FOLD):
        columns = [g * FOLD + i for i in range(FOLD)]
        left[:, lanes_from(g)] = flat_rows(rows_of(own, columns, 0))
        right[:, lanes_from(g)] = flat_rows(rows_of(own, columns, 1))
    vectors[...] = columns_of((norm_gain, norm_bias, out_gain, out_bias))
    field = field_of(pair)
    normed = layer_norm(field, vectors[:, 0:1], vectors[:, 3:4]).astype(BF16)
    gates[...] = sigmoid(dot(weight[0, :, 4 * WIDTH :].T, normed))
    fields[...] = field


def outgoing_kernel(other, left, right_own, product, right):
    core = core_index()
    for g in range(COLS // FOLD):
        columns = [g * FOLD + i for i in range(FOLD)]
        right[:, lanes_from(g)] = flat_rows(rows_of(other, columns, 1))
    for factor, parity in ((right_own, core), (right, 1 - core)):
        mixed = lax.dot_general(
            left[...], factor[...], (((1,), (1,)), ((), ())), preferred_element_type=F32
        )
        send_product(mixed, product, [2 * a + parity for a in range(PAIRS)])


def form_incoming(source, left, right):
    core = core_index()
    for g in range(COLS // FOLD):
        columns = [g * FOLD + i for i in range(FOLD)]
        right[:, lanes_from(g)] = flat_rows(rows_of(source, columns, 1))
    for g in range(PAIRS // FOLD):
        columns = [2 * (g * FOLD + i) + core for i in range(FOLD)]
        left[:, lanes_from(g)] = flat_rows(rows_of(source, columns, 0))


def incoming_own_kernel(own, fields, vectors, weight, left, right, gates):
    form_incoming(own, left, right)
    normed = layer_norm(fields[...], vectors[:, 1:2], vectors[:, 4:5]).astype(BF16)
    gates[...] = sigmoid(dot(weight[1, :, 4 * WIDTH :].T, normed))


def incoming_kernel(other, left_own, right_own, product, left, right):
    form_incoming(other, left, right)
    mixed = sum(
        lax.dot_general(a[...], b[...], (((0,), (0,)), ((), ())), preferred_element_type=F32)
        for a, b in ((left_own, right_own), (left, right))
    )
    send_product(mixed, product, range(COLS))


def call(kernel, outs, scratch, name, vmem=40, **more):
    return pl.pallas_call(
        kernel,
        out_shape=outs,
        scratch_shapes=scratch,
        compiler_params=pltpu.CompilerParams(vmem_limit_bytes=int(vmem * 1024 * 1024)),
        name=name,
        **more,
    )


def shape(*dims, dtype=BF16):
    return jax.ShapeDtypeStruct(dims, dtype)


def body(
    pair, norm_gain, norm_bias, proj_weight, out_gain, out_bias, out_weight, up_weight, down_weight
):
    flat = shape(WIDTH, STEPS * 128, dtype=F32)
    packed = shape(WIDTH, 2 * STEPS, 128)
    product = shape(WIDTH, STEPS, 128)
    packing = pltpu.VMEM((WIDTH * 2 * STEPS, 128), F32)
    unpacking = pltpu.VMEM((WIDTH * STEPS, 128), F32)
    blocks = (FOLD, STEPS, SIDE, WIDTH)

    pair = pair.reshape(blocks)
    operands = (pair, norm_gain, norm_bias)
    landing = [pltpu.VMEM(v.shape, v.dtype) for v in operands]
    landing += [pltpu.VMEM(proj_weight.shape[1:], BF16), packing, pltpu.SemaphoreType.DMA((4,))]
    hbm = pl.BlockSpec(memory_space=pltpu.HBM)
    factors = call(first_kernel, packed, landing, "first", 60, in_specs=[hbm] * 4)(
        *operands, proj_weight
    )
    own = exchange(factors)
    other = swap_cores(own)
    wide, square = (HALF, FULL), (HALF, HALF)
    outs = (shape(*wide), shape(*wide), flat, flat, shape(WIDTH, WIDTH, dtype=F32))
    left, right, gate, field, vectors = call(outgoing_own_kernel, outs, [], "outgoing_own")(
        own, pair, norm_gain, norm_bias, out_gain, out_bias, proj_weight
    )
    mixed = call(outgoing_kernel, product, [pltpu.VMEM(wide, BF16)], "outgoing")(
        other, left, right
    )
    factors, field = call(middle_kernel, (packed, flat), [packing, unpacking], "middle")(
        exchange(mixed), gate, field, vectors, proj_weight, out_weight
    )
    own = exchange(factors)
    other = swap_cores(own)
    outs = (shape(*square), shape(*wide), flat)
    left, right, gate = call(incoming_own_kernel, outs, [], "incoming_own")(
        own, field, vectors, proj_weight
    )
    forming = [pltpu.VMEM(square, BF16), pltpu.VMEM(wide, BF16)]
    mixed = call(incoming_kernel, product, forming, "incoming")(other, left, right)
    updated = call(last_kernel, shape(*blocks), [unpacking], "last")(
        exchange(mixed), gate, field, vectors, out_weight, up_weight, down_weight
    )
    return updated.reshape(FOLD * STEPS, SIDE, WIDTH)


def solution(mesh):
    placed = (P("row", "col", None), P(), P(), P(), P(), P(), P(), P(), P())
    return jax.shard_map(
        body, mesh=mesh, in_specs=placed, out_specs=P("row", "col", None), check_vma=False
    )
```

```python
import jax
import jax.numpy as jnp
from jax import lax
from jax.experimental import pallas as pl
from jax.experimental.pallas import tpu as pltpu
from jax.sharding import PartitionSpec as P

F32 = jnp.float32
BF16 = jnp.bfloat16
WIDTH = 128
SIDE = 32
STEPS = 8
FOLD = 4
PAIRS = 8
COLS = 16
HALF = PAIRS * SIDE
FULL = 2 * HALF

PARITY = [[(2 * a + core) * COLS + q for q in range(COLS) for a in range(PAIRS)] for core in (0, 1)]


def member(a, q):
    return q * PAIRS + a


def exchange(values):
    return lax.all_to_all(values, ("row", "col"), 0, 0, axis_index_groups=PARITY)


def swap_cores(values):
    return lax.ppermute(values, "row", [(i, i ^ 1) for i in range(2 * PAIRS)])


def core_index():
    return lax.rem(lax.axis_index("row"), 2)


def sigmoid(x):
    return 0.5 + 0.5 * jnp.tanh(0.5 * x)


def layer_norm(values, gain, bias):
    mean = jnp.mean(values, axis=0, keepdims=True)
    centred = values - mean
    var = jnp.mean(centred * centred, axis=0, keepdims=True)
    return centred * lax.rsqrt(var + 1e-05) * gain + bias


def dot(a, b):
    return lax.dot_general(a, b, (((1,), (0,)), ((), ())), preferred_element_type=F32)


def finish(field, mixed, gain, bias, weight, gate):
    mixnorm = layer_norm(mixed, gain, bias).astype(BF16)
    return field + gate * dot(weight, mixnorm)


def take_mixed(mixed, scratch):
    scratch[...] = mixed[...].astype(F32).reshape(WIDTH * STEPS, 128)
    steps = [scratch[pl.ds(step, WIDTH, stride=STEPS), :] for step in range(STEPS)]
    return jnp.concatenate(steps, axis=1)


def field_of(pair):
    rows = pair[...].astype(F32)
    steps = [rows[:, i].reshape(FOLD * SIDE, WIDTH).T for i in range(STEPS)]
    return jnp.concatenate(steps, axis=1)


def columns_of(refs):
    rows = jnp.concatenate([ref[...] for ref in refs], axis=0)
    rest = jnp.zeros((WIDTH - rows.shape[0], WIDTH), F32)
    return jnp.concatenate([rows, rest], axis=0).T


def factors_of(proj):
    h = WIDTH
    left = sigmoid(proj[:h]) * proj[h : 2 * h]
    right = sigmoid(proj[2 * h : 3 * h]) * proj[3 * h : 4 * h]
    return left, right


def put_factors(scratch, left, right, factors):
    for step in range(STEPS):
        lanes = slice(step * 128, (step + 1) * 128)
        scratch[pl.ds(step, WIDTH, stride=2 * STEPS), :] = left[:, lanes]
        scratch[pl.ds(step + STEPS, WIDTH, stride=2 * STEPS), :] = right[:, lanes]
    factors[...] = scratch[...].reshape(WIDTH, 2 * STEPS, 128).astype(BF16)


def first_kernel(pair, norm_gain, norm_bias, weight, factors, scratch):
    vectors = columns_of((norm_gain, norm_bias))
    normed = layer_norm(field_of(pair), vectors[:, 0:1], vectors[:, 3:4]).astype(BF16)
    put_factors(scratch, *factors_of(dot(weight[...], normed)), factors)


def middle_kernel(
    mixed, gates, fields, vectors, weight, out_weight, factors, fields_out, scratch, product
):
    gain, bias = vectors[:, 1:2], vectors[:, 4:5]
    mix_gain, mix_bias = vectors[:, 6:7], vectors[:, 8:9]
    field = finish(
        fields[...], take_mixed(mixed, product), mix_gain, mix_bias, out_weight[0].T, gates[...]
    )
    normed = layer_norm(field, gain, bias).astype(BF16)
    put_factors(scratch, *factors_of(dot(weight[1, :, : 4 * WIDTH].T, normed)), factors)
    fields_out[...] = field


def last_kernel(mixed, gates, fields, vectors, out_weight, up, down, updated, product):
    gain, bias = vectors[:, 2:3], vectors[:, 5:6]
    mix_gain, mix_bias = vectors[:, 7:8], vectors[:, 9:10]
    inner = down.shape[0]
    field = finish(
        fields[...], take_mixed(mixed, product), mix_gain, mix_bias, out_weight[1].T, gates[...]
    )
    expanded = dot(up[...].T, layer_norm(field, gain, bias).astype(BF16))
    wide = expanded[:inner]
    act = (wide * sigmoid(wide) * expanded[inner:]).astype(BF16)
    field = field + dot(down[...].T, act)
    for i in range(STEPS):
        block = field[:, i * 128 : (i + 1) * 128].T.reshape(FOLD, SIDE, WIDTH)
        updated[:, i] = block.astype(BF16)


def turn(tiles):
    lane = lax.broadcasted_iota(jnp.int32, tiles[0].shape, 1)
    low = lane < 64
    even = (lane & 32) == 0

    def far(a, b):
        moved = pltpu.roll(jnp.where(low, b, a), 64, 1)
        return jnp.where(low, a, moved), jnp.where(low, moved, b)

    def near(a, b):
        return (
            jnp.where(even, a, pltpu.roll(b, 32, 1)),
            jnp.where(even, pltpu.roll(a, 96, 1), b),
        )

    a, b, c, d = tiles
    a, c = far(a, c)
    b, d = far(b, d)
    return *near(a, b), *near(c, d)


def lanes_from(g):
    return slice(g * 128, (g + 1) * 128)


def rows_of(source, columns, half):
    rows = slice(half * STEPS, (half + 1) * STEPS)
    tiles = [
        source[pl.ds(member(0, q), PAIRS), rows, :].astype(F32).reshape(PAIRS * STEPS, 128)
        for q in columns
    ]
    tiles = [tile.reshape(PAIRS, 1, STEPS, 128) for tile in turn(tiles)]
    return jnp.concatenate(tiles, axis=1)


def flat_rows(block):
    return block.reshape(HALF, 128).astype(BF16)


def send_product(mixed, product, columns):
    mixed = mixed.reshape(PAIRS, FOLD, STEPS, SIDE * len(columns))
    for g in range(len(columns) // FOLD):
        tiles = [mixed[:, i, :, lanes_from(g)].reshape(PAIRS * STEPS, 128) for i in range(FOLD)]
        for i, tile in enumerate(turn(tiles)):
            rows = pl.ds(member(0, columns[g * FOLD + i]), PAIRS)
            product[rows] = tile.reshape(PAIRS, STEPS, 128).astype(BF16)


def dot_rows(left, right):
    return lax.dot_general(
        left[...], right[...], (((1,), (1,)), ((), ())), preferred_element_type=F32
    )


def dot_columns(left, right):
    return lax.dot_general(
        left[...], right[...], (((0,), (0,)), ((), ())), preferred_element_type=F32
    )


def outgoing_own_kernel(
    own, pair, norm_gain, norm_bias, out_gain, out_bias, weight,
    left, own_product, gates, fields, vectors, right,
):
    for g in range(COLS // FOLD):
        columns = [g * FOLD + i for i in range(FOLD)]
        left[:, lanes_from(g)] = flat_rows(rows_of(own, columns, 0))
        right[:, lanes_from(g)] = flat_rows(rows_of(own, columns, 1))
    send_product(dot_rows(left, right), own_product, range(PAIRS))
    vectors[...] = columns_of((norm_gain, norm_bias, out_gain, out_bias))
    field = field_of(pair)
    normed = layer_norm(field, vectors[:, 0:1], vectors[:, 3:4]).astype(BF16)
    gates[...] = sigmoid(dot(weight[0, :, 4 * WIDTH :].T, normed))
    fields[...] = field


def outgoing_kernel(other, left, own_product, product, right):
    core = core_index()
    for g in range(COLS // FOLD):
        columns = [g * FOLD + i for i in range(FOLD)]
        right[:, lanes_from(g)] = flat_rows(rows_of(other, columns, 0))
    for a in range(PAIRS):
        rows = pl.ds(member(0, 2 * a + core), PAIRS)
        product[rows] = own_product[member(0, a) : member(0, a + 1)]
    send_product(dot_rows(left, right), product, [2 * a + 1 - core for a in range(PAIRS)])


def form_incoming(source, left, right):
    core = core_index()
    for g in range(COLS // FOLD):
        columns = [g * FOLD + i for i in range(FOLD)]
        right[:, lanes_from(g)] = flat_rows(rows_of(source, columns, 1))
    for g in range(PAIRS // FOLD):
        columns = [2 * (g * FOLD + i) + core for i in range(FOLD)]
        left[:, lanes_from(g)] = flat_rows(rows_of(source, columns, 0))


def incoming_own_kernel(own, fields, vectors, weight, own_mixed, gates, left, right):
    form_incoming(own, left, right)
    own_mixed[...] = dot_columns(left, right)
    normed = layer_norm(fields[...], vectors[:, 1:2], vectors[:, 4:5]).astype(BF16)
    gates[...] = sigmoid(dot(weight[1, :, 4 * WIDTH :].T, normed))


def incoming_kernel(other, own_mixed, product, left, right):
    form_incoming(other, left, right)
    send_product(own_mixed[...] + dot_columns(left, right), product, range(COLS))


def call(kernel, outs, scratch, name, vmem=40, **more):
    return pl.pallas_call(
        kernel,
        out_shape=outs,
        scratch_shapes=scratch,
        compiler_params=pltpu.CompilerParams(vmem_limit_bytes=int(vmem * 1024 * 1024)),
        name=name,
        **more,
    )


def shape(*dims, dtype=BF16):
    return jax.ShapeDtypeStruct(dims, dtype)


def body(
    pair, norm_gain, norm_bias, proj_weight, out_gain, out_bias, out_weight, up_weight, down_weight
):
    flat = shape(WIDTH, STEPS * 128, dtype=F32)
    packed = shape(WIDTH, 2 * STEPS, 128)
    product = shape(WIDTH, STEPS, 128)
    packing = pltpu.VMEM((WIDTH * 2 * STEPS, 128), F32)
    unpacking = pltpu.VMEM((WIDTH * STEPS, 128), F32)
    blocks = (FOLD, STEPS, SIDE, WIDTH)

    pair = pair.reshape(blocks)
    factors = call(first_kernel, packed, [packing], "first")(
        pair, norm_gain, norm_bias, proj_weight[0, :, : 4 * WIDTH].T
    )
    own = exchange(factors)
    other = swap_cores(own[:, STEPS:])
    wide, square = (HALF, FULL), (HALF, HALF)
    outs = (shape(*wide), shape(WIDTH // 2, STEPS, 128), flat, flat)
    factor, square = pltpu.VMEM(wide, BF16), pltpu.VMEM(square, BF16)
    left, own_product, gate, field, vectors = call(
        outgoing_own_kernel, (*outs, shape(WIDTH, WIDTH, dtype=F32)), [factor], "outgoing_own"
    )(own, pair, norm_gain, norm_bias, out_gain, out_bias, proj_weight)
    mixed = call(outgoing_kernel, product, [factor], "outgoing")(other, left, own_product)
    factors, field = call(middle_kernel, (packed, flat), [packing, unpacking], "middle")(
        exchange(mixed), gate, field, vectors, proj_weight, out_weight
    )
    own = exchange(factors)
    other = swap_cores(own)
    outs = (shape(*wide, dtype=F32), flat)
    own_mixed, gate = call(incoming_own_kernel, outs, [square, factor], "incoming_own")(
        own, field, vectors, proj_weight
    )
    mixed = call(incoming_kernel, product, [square, factor], "incoming")(other, own_mixed)
    updated = call(last_kernel, shape(*blocks), [unpacking], "last")(
        exchange(mixed), gate, field, vectors, out_weight, up_weight, down_weight
    )
    return updated.reshape(FOLD * STEPS, SIDE, WIDTH)


def solution(mesh):
    placed = (P("row", "col", None), P(), P(), P(), P(), P(), P(), P(), P())
    return jax.shard_map(
        body, mesh=mesh, in_specs=placed, out_specs=P("row", "col", None), check_vma=False
    )
```

```python
import jax
import jax.numpy as jnp
from jax import lax
from jax.experimental import pallas as pl
from jax.experimental.pallas import tpu as pltpu
from jax.sharding import PartitionSpec as P

F32 = jnp.float32
BF16 = jnp.bfloat16
WIDTH = 128
SIDE = 32
STEPS = 8
FOLD = 4
PAIRS = 8
COLS = 16
HALF = PAIRS * SIDE
FULL = 2 * HALF

PARITY = [[(2 * a + core) * COLS + q for q in range(COLS) for a in range(PAIRS)] for core in (0, 1)]


def member(a, q):
    return q * PAIRS + a


def exchange(values):
    return lax.all_to_all(values, ("row", "col"), 0, 0, axis_index_groups=PARITY)


def swap_cores(values):
    return lax.ppermute(values, "row", [(i, i ^ 1) for i in range(2 * PAIRS)])


def core_index():
    return lax.rem(lax.axis_index("row"), 2)


def halved(weight):
    return weight * jnp.asarray(0.5, weight.dtype)


def sigmoid_of_double(half):
    return 0.5 + 0.5 * jnp.tanh(half)


def times_sigmoid_of_double(half, other):
    return other * jnp.tanh(half) + other


def layer_norm(values, gain, bias):
    mean = jnp.mean(values, axis=0, keepdims=True)
    centred = values - mean
    var = jnp.mean(centred * centred, axis=0, keepdims=True)
    return centred * lax.rsqrt(var + 1e-05) * gain + bias


def dot(a, b):
    return lax.dot_general(a, b, (((1,), (0,)), ((), ())), preferred_element_type=F32)


def finish(field, mixed, gain, bias, weight, gate):
    mixnorm = layer_norm(mixed, gain, bias).astype(BF16)
    return field + gate * dot(weight, mixnorm)


def take_mixed(mixed, scratch):
    scratch[: WIDTH * STEPS] = mixed[...].astype(F32).reshape(WIDTH * STEPS, 128)
    steps = [scratch[pl.ds(step, WIDTH, stride=STEPS), :] for step in range(STEPS)]
    return jnp.concatenate(steps, axis=1)


def field_of(pair):
    rows = pair[...].astype(F32)
    steps = [rows[:, i].reshape(FOLD * SIDE, WIDTH).T for i in range(STEPS)]
    return jnp.concatenate(steps, axis=1)


def columns_of(refs):
    rows = jnp.concatenate([ref[...] for ref in refs], axis=0)
    rest = jnp.zeros((WIDTH - rows.shape[0], WIDTH), F32)
    return jnp.concatenate([rows, rest], axis=0).T


def factors_of(proj):
    h = WIDTH
    left = times_sigmoid_of_double(proj[:h], proj[h : 2 * h])
    right = times_sigmoid_of_double(proj[2 * h : 3 * h], proj[3 * h : 4 * h])
    return left, right


def put_factors(scratch, left, right, factors):
    for step in range(STEPS):
        lanes = slice(step * 128, (step + 1) * 128)
        scratch[pl.ds(step, WIDTH, stride=2 * STEPS), :] = left[:, lanes]
        scratch[pl.ds(step + STEPS, WIDTH, stride=2 * STEPS), :] = right[:, lanes]
    rows = scratch[: WIDTH * 2 * STEPS]
    factors[...] = rows.reshape(WIDTH, 2 * STEPS, 128).astype(BF16)


def first_kernel(pair, norm_gain, norm_bias, weight, factors, scratch):
    vectors = columns_of((norm_gain, norm_bias))
    normed = layer_norm(field_of(pair), vectors[:, 0:1], vectors[:, 3:4]).astype(BF16)
    put_factors(scratch, *factors_of(dot(halved(weight[...]), normed)), factors)


def middle_kernel(
    mixed, gates, fields, vectors, weight, out_weight, factors, fields_out, scratch, product
):
    gain, bias = vectors[:, 1:2], vectors[:, 4:5]
    mix_gain, mix_bias = vectors[:, 6:7], vectors[:, 8:9]
    field = finish(
        fields[...], take_mixed(mixed, product), mix_gain, mix_bias, out_weight[0].T, gates[...]
    )
    normed = layer_norm(field, gain, bias).astype(BF16)
    put_factors(scratch, *factors_of(dot(halved(weight[1, :, : 4 * WIDTH]).T, normed)), factors)
    fields_out[...] = field


def last_kernel(mixed, gates, fields, vectors, out_weight, up, down, updated, product):
    gain, bias = vectors[:, 2:3], vectors[:, 5:6]
    mix_gain, mix_bias = vectors[:, 7:8], vectors[:, 9:10]
    inner = down.shape[0]
    field = finish(
        fields[...], take_mixed(mixed, product), mix_gain, mix_bias, out_weight[1].T, gates[...]
    )
    tnorm = layer_norm(field, gain, bias).astype(BF16)
    half = dot(halved(up[:, :inner]).T, tnorm)
    act = (times_sigmoid_of_double(half, half) * dot(up[:, inner:].T, tnorm)).astype(BF16)
    field = field + dot(down[...].T, act)
    for i in range(STEPS):
        block = field[:, i * 128 : (i + 1) * 128].T.reshape(FOLD, SIDE, WIDTH)
        updated[:, i] = block.astype(BF16)


def turn(tiles):
    lane = lax.broadcasted_iota(jnp.int32, tiles[0].shape, 1)
    low = lane < 64
    even = (lane & 32) == 0

    def far(a, b):
        moved = pltpu.roll(jnp.where(low, b, a), 64, 1)
        return jnp.where(low, a, moved), jnp.where(low, moved, b)

    def near(a, b):
        return (
            jnp.where(even, a, pltpu.roll(b, 32, 1)),
            jnp.where(even, pltpu.roll(a, 96, 1), b),
        )

    a, b, c, d = tiles
    a, c = far(a, c)
    b, d = far(b, d)
    return *near(a, b), *near(c, d)


def lanes_from(g):
    return slice(g * 128, (g + 1) * 128)


def rows_of(source, columns, half):
    rows = slice(half * STEPS, (half + 1) * STEPS)
    tiles = [
        source[pl.ds(member(0, q), PAIRS), rows, :].astype(F32).reshape(PAIRS * STEPS, 128)
        for q in columns
    ]
    tiles = [tile.reshape(PAIRS, 1, STEPS, 128) for tile in turn(tiles)]
    return jnp.concatenate(tiles, axis=1)


def flat_rows(block):
    return block.reshape(HALF, 128).astype(BF16)


def send_product(mixed, product, columns):
    mixed = mixed.reshape(PAIRS, FOLD, STEPS, SIDE * len(columns))
    for g in range(len(columns) // FOLD):
        tiles = [mixed[:, i, :, lanes_from(g)].reshape(PAIRS * STEPS, 128) for i in range(FOLD)]
        for i, tile in enumerate(turn(tiles)):
            rows = pl.ds(member(0, columns[g * FOLD + i]), PAIRS)
            product[rows] = tile.reshape(PAIRS, STEPS, 128).astype(BF16)


def dot_rows(left, right):
    return lax.dot_general(
        left[...], right[...], (((1,), (1,)), ((), ())), preferred_element_type=F32
    )


def dot_columns(left, right):
    return lax.dot_general(
        left[...], right[...], (((0,), (0,)), ((), ())), preferred_element_type=F32
    )


def outgoing_own_kernel(
    own, pair, norm_gain, norm_bias, out_gain, out_bias, weight,
    left, own_product, gates, fields, vectors, right,
):
    for g in range(COLS // FOLD):
        columns = [g * FOLD + i for i in range(FOLD)]
        left[:, lanes_from(g)] = flat_rows(rows_of(own, columns, 0))
        right[:, lanes_from(g)] = flat_rows(rows_of(own, columns, 1))
    send_product(dot_rows(left, right), own_product, range(PAIRS))
    vectors[...] = columns_of((norm_gain, norm_bias, out_gain, out_bias))
    field = field_of(pair)
    normed = layer_norm(field, vectors[:, 0:1], vectors[:, 3:4]).astype(BF16)
    gates[...] = sigmoid_of_double(dot(halved(weight[0, :, 4 * WIDTH :]).T, normed))
    fields[...] = field


def outgoing_kernel(other, left, own_product, product, right):
    core = core_index()
    for g in range(COLS // FOLD):
        columns = [g * FOLD + i for i in range(FOLD)]
        right[:, lanes_from(g)] = flat_rows(rows_of(other, columns, 0))
    for a in range(PAIRS):
        rows = pl.ds(member(0, 2 * a + core), PAIRS)
        product[rows] = own_product[member(0, a) : member(0, a + 1)]
    send_product(dot_rows(left, right), product, [2 * a + 1 - core for a in range(PAIRS)])


def form_incoming(source, left, right):
    core = core_index()
    for g in range(COLS // FOLD):
        columns = [g * FOLD + i for i in range(FOLD)]
        right[:, lanes_from(g)] = flat_rows(rows_of(source, columns, 1))
    for g in range(PAIRS // FOLD):
        columns = [2 * (g * FOLD + i) + core for i in range(FOLD)]
        left[:, lanes_from(g)] = flat_rows(rows_of(source, columns, 0))


def incoming_own_kernel(own, fields, vectors, weight, own_mixed, gates, left, right):
    form_incoming(own, left, right)
    own_mixed[...] = dot_columns(left, right)
    normed = layer_norm(fields[...], vectors[:, 1:2], vectors[:, 4:5]).astype(BF16)
    gates[...] = sigmoid_of_double(dot(halved(weight[1, :, 4 * WIDTH :]).T, normed))


def incoming_kernel(other, own_mixed, product, left, right):
    form_incoming(other, left, right)
    send_product(own_mixed[...] + dot_columns(left, right), product, range(COLS))


def call(kernel, outs, scratch, name, vmem=40, **more):
    return pl.pallas_call(
        kernel,
        out_shape=outs,
        scratch_shapes=scratch,
        compiler_params=pltpu.CompilerParams(vmem_limit_bytes=int(vmem * 1024 * 1024)),
        name=name,
        **more,
    )


def shape(*dims, dtype=BF16):
    return jax.ShapeDtypeStruct(dims, dtype)


def body(
    pair, norm_gain, norm_bias, proj_weight, out_gain, out_bias, out_weight, up_weight, down_weight
):
    flat = shape(WIDTH, STEPS * 128, dtype=F32)
    packed = shape(WIDTH, 2 * STEPS, 128)
    product = shape(WIDTH, STEPS, 128)
    packing = pltpu.VMEM(((WIDTH + 1) * 2 * STEPS, 128), F32)
    unpacking = pltpu.VMEM(((WIDTH + 1) * STEPS, 128), F32)
    blocks = (FOLD, STEPS, SIDE, WIDTH)

    pair = pair.reshape(blocks)
    factors = call(first_kernel, packed, [packing], "first")(
        pair, norm_gain, norm_bias, proj_weight[0, :, : 4 * WIDTH].T
    )
    own = exchange(factors)
    other = swap_cores(own[:, STEPS:])
    wide, square = (HALF, FULL), (HALF, HALF)
    outs = (shape(*wide), shape(WIDTH // 2, STEPS, 128), flat, flat)
    factor, square = pltpu.VMEM(wide, BF16), pltpu.VMEM(square, BF16)
    left, own_product, gate, field, vectors = call(
        outgoing_own_kernel, (*outs, shape(WIDTH, WIDTH, dtype=F32)), [factor], "outgoing_own"
    )(own, pair, norm_gain, norm_bias, out_gain, out_bias, proj_weight)
    mixed = call(outgoing_kernel, product, [factor], "outgoing")(other, left, own_product)
    factors, field = call(middle_kernel, (packed, flat), [packing, unpacking], "middle")(
        exchange(mixed), gate, field, vectors, proj_weight, out_weight
    )
    own = exchange(factors)
    other = swap_cores(own)
    outs = (shape(*wide, dtype=F32), flat)
    own_mixed, gate = call(incoming_own_kernel, outs, [square, factor], "incoming_own")(
        own, field, vectors, proj_weight
    )
    mixed = call(incoming_kernel, product, [square, factor], "incoming")(other, own_mixed)
    updated = call(last_kernel, shape(*blocks), [unpacking], "last")(
        exchange(mixed), gate, field, vectors, out_weight, up_weight, down_weight
    )
    return updated.reshape(FOLD * STEPS, SIDE, WIDTH)


def solution(mesh):
    placed = (P("row", "col", None), P(), P(), P(), P(), P(), P(), P(), P())
    return jax.shard_map(
        body, mesh=mesh, in_specs=placed, out_specs=P("row", "col", None), check_vma=False
    )
```

```python
import jax
import jax.numpy as jnp
from jax import lax
from jax.experimental import pallas as pl
from jax.experimental.pallas import tpu as pltpu
from jax.sharding import PartitionSpec as P

F32 = jnp.float32
BF16 = jnp.bfloat16
WIDTH = 128
SIDE = 32
STEPS = 8
FOLD = 4
PAIRS = 8
COLS = 16
HALF = PAIRS * SIDE
FULL = 2 * HALF

PARITY = [[(2 * a + core) * COLS + q for q in range(COLS) for a in range(PAIRS)] for core in (0, 1)]


def member(a, q):
    return q * PAIRS + a


def exchange(values):
    return lax.all_to_all(values, ("row", "col"), 0, 0, axis_index_groups=PARITY)


def swap_cores(values):
    return lax.ppermute(values, "row", [(i, i ^ 1) for i in range(2 * PAIRS)])


def core_index():
    return lax.rem(lax.axis_index("row"), 2)


def halved(weight):
    return weight * jnp.asarray(0.5, weight.dtype)


def sigmoid_of_double(half):
    return 0.5 + 0.5 * jnp.tanh(half)


def times_sigmoid_of_double(half, other):
    return other * jnp.tanh(half) + other


def layer_norm(values, gain, bias):
    mean = jnp.mean(values, axis=0, keepdims=True)
    centred = values - mean
    var = jnp.mean(centred * centred, axis=0, keepdims=True)
    return centred * lax.rsqrt(var + 1e-05) * gain + bias


def dot(a, b):
    return lax.dot_general(a, b, (((1,), (0,)), ((), ())), preferred_element_type=F32)


def finish(field, mixed, gain, bias, weight, gate):
    mixnorm = layer_norm(mixed, gain, bias).astype(BF16)
    return field + gate * dot(weight, mixnorm)


def take_mixed(mixed, scratch):
    scratch[: WIDTH * STEPS] = mixed[...].astype(F32).reshape(WIDTH * STEPS, 128)
    steps = [scratch[pl.ds(step, WIDTH, stride=STEPS), :] for step in range(STEPS)]
    return jnp.concatenate(steps, axis=1)


def field_of(pair):
    rows = pair[...].astype(F32)
    steps = [rows[:, i].reshape(FOLD * SIDE, WIDTH).T for i in range(STEPS)]
    return jnp.concatenate(steps, axis=1)


def columns_of(refs):
    rows = jnp.concatenate([ref[...] for ref in refs], axis=0)
    rest = jnp.zeros((WIDTH - rows.shape[0], WIDTH), F32)
    return jnp.concatenate([rows, rest], axis=0).T


def factors_of(proj):
    h = WIDTH
    left = times_sigmoid_of_double(proj[:h], proj[h : 2 * h])
    right = times_sigmoid_of_double(proj[2 * h : 3 * h], proj[3 * h : 4 * h])
    return left, right


def put_factors(scratch, left, right, factors):
    for step in range(STEPS):
        lanes = slice(step * 128, (step + 1) * 128)
        scratch[pl.ds(step, WIDTH, stride=2 * STEPS), :] = left[:, lanes]
        scratch[pl.ds(step + STEPS, WIDTH, stride=2 * STEPS), :] = right[:, lanes]
    rows = scratch[: WIDTH * 2 * STEPS]
    factors[...] = rows.reshape(WIDTH, 2 * STEPS, 128).astype(BF16)


def first_kernel(pair, norm_gain, norm_bias, weight, factors, scratch):
    vectors = columns_of((norm_gain, norm_bias))
    normed = layer_norm(field_of(pair), vectors[:, 0:1], vectors[:, 3:4]).astype(BF16)
    put_factors(scratch, *factors_of(dot(halved(weight[: 4 * WIDTH]), normed)), factors)


def middle_kernel(
    mixed, gates, fields, vectors, weight, out_weight, factors, fields_out, scratch, product
):
    gain, bias = vectors[:, 1:2], vectors[:, 4:5]
    mix_gain, mix_bias = vectors[:, 6:7], vectors[:, 8:9]
    field = finish(
        fields[...], take_mixed(mixed, product), mix_gain, mix_bias, out_weight[0].T, gates[...]
    )
    normed = layer_norm(field, gain, bias).astype(BF16)
    put_factors(scratch, *factors_of(dot(halved(weight[1, :, : 4 * WIDTH]).T, normed)), factors)
    fields_out[...] = field


def last_kernel(mixed, gates, fields, vectors, out_weight, up, down, updated, product):
    gain, bias = vectors[:, 2:3], vectors[:, 5:6]
    mix_gain, mix_bias = vectors[:, 7:8], vectors[:, 9:10]
    inner = down.shape[0]
    field = finish(
        fields[...], take_mixed(mixed, product), mix_gain, mix_bias, out_weight[1].T, gates[...]
    )
    tnorm = layer_norm(field, gain, bias).astype(BF16)
    half = dot(halved(up[:, :inner]).T, tnorm)
    act = (times_sigmoid_of_double(half, half) * dot(up[:, inner:].T, tnorm)).astype(BF16)
    field = field + dot(down[...].T, act)
    for i in range(STEPS):
        block = field[:, i * 128 : (i + 1) * 128].T.reshape(FOLD, SIDE, WIDTH)
        updated[:, i] = block.astype(BF16)


def turn(tiles):
    lane = lax.broadcasted_iota(jnp.int32, tiles[0].shape, 1)
    low = lane < 64
    even = (lane & 32) == 0

    def far(a, b):
        moved = pltpu.roll(jnp.where(low, b, a), 64, 1)
        return jnp.where(low, a, moved), jnp.where(low, moved, b)

    def near(a, b):
        return (
            jnp.where(even, a, pltpu.roll(b, 32, 1)),
            jnp.where(even, pltpu.roll(a, 96, 1), b),
        )

    a, b, c, d = tiles
    a, c = far(a, c)
    b, d = far(b, d)
    return *near(a, b), *near(c, d)


def lanes_from(g):
    return slice(g * 128, (g + 1) * 128)


def rows_of(source, columns, half):
    rows = slice(half * STEPS, (half + 1) * STEPS)
    tiles = [source[pl.ds(member(0, q), PAIRS)].astype(F32)[:, rows] for q in columns]
    tiles = turn([tile.reshape(PAIRS * STEPS, 128) for tile in tiles])
    tiles = [tile.reshape(PAIRS, 1, STEPS, 128) for tile in tiles]
    return jnp.concatenate(tiles, axis=1)


def flat_rows(block):
    return block.reshape(HALF, 128).astype(BF16)


def send_product(mixed, product, columns):
    mixed = mixed.reshape(PAIRS, FOLD, STEPS, SIDE * len(columns))
    for g in range(len(columns) // FOLD):
        tiles = [mixed[:, i, :, lanes_from(g)].reshape(PAIRS * STEPS, 128) for i in range(FOLD)]
        for i, tile in enumerate(turn(tiles)):
            rows = pl.ds(member(0, columns[g * FOLD + i]), PAIRS)
            product[rows] = tile.reshape(PAIRS, STEPS, 128).astype(BF16)


def dot_rows(left, right):
    return lax.dot_general(
        left[...], right[...], (((1,), (1,)), ((), ())), preferred_element_type=F32
    )


def dot_columns(left, right):
    return lax.dot_general(
        left[...], right[...], (((0,), (0,)), ((), ())), preferred_element_type=F32
    )


def outgoing_own_kernel(
    own, pair, norm_gain, norm_bias, out_gain, out_bias, weight,
    left, own_product, gates, fields, vectors, right,
):
    for g in range(COLS // FOLD):
        columns = [g * FOLD + i for i in range(FOLD)]
        left[:, lanes_from(g)] = flat_rows(rows_of(own, columns, 0))
        right[:, lanes_from(g)] = flat_rows(rows_of(own, columns, 1))
    send_product(dot_rows(left, right), own_product, range(PAIRS))
    vectors[...] = columns_of((norm_gain, norm_bias, out_gain, out_bias))
    field = field_of(pair)
    normed = layer_norm(field, vectors[:, 0:1], vectors[:, 3:4]).astype(BF16)
    gates[...] = sigmoid_of_double(dot(halved(weight[4 * WIDTH :]), normed))
    fields[...] = field


def outgoing_kernel(other, left, own_product, product, right):
    core = core_index()
    for g in range(COLS // FOLD):
        columns = [g * FOLD + i for i in range(FOLD)]
        right[:, lanes_from(g)] = flat_rows(rows_of(other, columns, 0))
    for a in range(PAIRS):
        rows = pl.ds(member(0, 2 * a + core), PAIRS)
        product[rows] = own_product[member(0, a) : member(0, a + 1)]
    send_product(dot_rows(left, right), product, [2 * a + 1 - core for a in range(PAIRS)])


def form_incoming(source, left, right):
    core = core_index()
    for g in range(COLS // FOLD):
        columns = [g * FOLD + i for i in range(FOLD)]
        right[:, lanes_from(g)] = flat_rows(rows_of(source, columns, 1))
    for g in range(PAIRS // FOLD):
        columns = [2 * (g * FOLD + i) + core for i in range(FOLD)]
        left[:, lanes_from(g)] = flat_rows(rows_of(source, columns, 0))


def incoming_own_kernel(own, fields, vectors, weight, own_mixed, gates, left, right):
    form_incoming(own, left, right)
    own_mixed[...] = dot_columns(left, right)
    normed = layer_norm(fields[...], vectors[:, 1:2], vectors[:, 4:5]).astype(BF16)
    gates[...] = sigmoid_of_double(dot(halved(weight[1, :, 4 * WIDTH :]).T, normed))


def incoming_kernel(other, own_mixed, product, left, right):
    form_incoming(other, left, right)
    send_product(own_mixed[...] + dot_columns(left, right), product, range(COLS))


def call(kernel, outs, scratch, name, vmem=40, **more):
    return pl.pallas_call(
        kernel,
        out_shape=outs,
        scratch_shapes=scratch,
        compiler_params=pltpu.CompilerParams(vmem_limit_bytes=int(vmem * 1024 * 1024)),
        name=name,
        **more,
    )


def shape(*dims, dtype=BF16):
    return jax.ShapeDtypeStruct(dims, dtype)


def body(
    pair, norm_gain, norm_bias, proj_weight, out_gain, out_bias, out_weight, up_weight, down_weight
):
    flat = shape(WIDTH, STEPS * 128, dtype=F32)
    packed = shape(WIDTH, 2 * STEPS, 128)
    product = shape(WIDTH, STEPS, 128)
    packing = pltpu.VMEM(((WIDTH + 1) * 2 * STEPS, 128), F32)
    unpacking = pltpu.VMEM(((WIDTH + 1) * STEPS, 128), F32)
    blocks = (FOLD, STEPS, SIDE, WIDTH)

    pair = pair.reshape(blocks)
    first_weight = proj_weight[0].T
    factors = call(first_kernel, packed, [packing], "first")(
        pair, norm_gain, norm_bias, first_weight
    )
    own = exchange(factors)
    other = swap_cores(own[:, STEPS:])
    wide, square = (HALF, FULL), (HALF, HALF)
    outs = (shape(*wide), shape(WIDTH // 2, STEPS, 128), flat, flat)
    factor, square = pltpu.VMEM(wide, BF16), pltpu.VMEM(square, BF16)
    left, own_product, gate, field, vectors = call(
        outgoing_own_kernel, (*outs, shape(WIDTH, WIDTH, dtype=F32)), [factor], "outgoing_own"
    )(own, pair, norm_gain, norm_bias, out_gain, out_bias, first_weight)
    mixed = call(outgoing_kernel, product, [factor], "outgoing")(other, left, own_product)
    factors, field = call(middle_kernel, (packed, flat), [packing, unpacking], "middle")(
        exchange(mixed), gate, field, vectors, proj_weight, out_weight
    )
    own = exchange(factors)
    other = swap_cores(own)
    outs = (shape(*wide, dtype=F32), flat)
    own_mixed, gate = call(incoming_own_kernel, outs, [square, factor], "incoming_own")(
        own, field, vectors, proj_weight
    )
    mixed = call(incoming_kernel, product, [square, factor], "incoming")(other, own_mixed)
    updated = call(last_kernel, shape(*blocks), [unpacking], "last")(
        exchange(mixed), gate, field, vectors, out_weight, up_weight, down_weight
    )
    return updated.reshape(FOLD * STEPS, SIDE, WIDTH)


def solution(mesh):
    placed = (P("row", "col", None), P(), P(), P(), P(), P(), P(), P(), P())
    return jax.shard_map(
        body, mesh=mesh, in_specs=placed, out_specs=P("row", "col", None), check_vma=False
    )
```

```python
import jax
import jax.numpy as jnp
from jax import lax
from jax.experimental import pallas as pl
from jax.experimental.pallas import tpu as pltpu
from jax.sharding import PartitionSpec as P

F32 = jnp.float32
BF16 = jnp.bfloat16
WIDTH = 128
SIDE = 32
STEPS = 8
FOLD = 4
PAIRS = 8
COLS = 16
HALF = PAIRS * SIDE
FULL = 2 * HALF

PARITY = [[(2 * a + core) * COLS + q for q in range(COLS) for a in range(PAIRS)] for core in (0, 1)]


def member(a, q):
    return q * PAIRS + a


def exchange(values):
    return lax.all_to_all(values, ("row", "col"), 0, 0, axis_index_groups=PARITY)


def swap_cores(values):
    return lax.ppermute(values, "row", [(i, i ^ 1) for i in range(2 * PAIRS)])


def core_index():
    return lax.rem(lax.axis_index("row"), 2)


def halved(weight):
    return weight * jnp.asarray(0.5, weight.dtype)


def sigmoid_of_double(half):
    return 0.5 + 0.5 * jnp.tanh(half)


def times_sigmoid_of_double(half, other):
    return other * jnp.tanh(half) + other


def layer_norm(values, gain, bias):
    mean = jnp.mean(values, axis=0, keepdims=True)
    centred = values - mean
    var = jnp.mean(centred * centred, axis=0, keepdims=True)
    return centred * lax.rsqrt(var + 1e-05) * gain + bias


def dot(a, b):
    return lax.dot_general(a, b, (((1,), (0,)), ((), ())), preferred_element_type=F32)


def finish(field, mixed, gain, bias, weight, gate):
    mixnorm = layer_norm(mixed, gain, bias).astype(BF16)
    return field + gate * dot(weight, mixnorm)


def take_mixed(mixed, scratch):
    scratch[: WIDTH * STEPS] = mixed[...].astype(F32).reshape(WIDTH * STEPS, 128)
    steps = [scratch[pl.ds(step, WIDTH, stride=STEPS), :] for step in range(STEPS)]
    return jnp.concatenate(steps, axis=1)


def field_of(pair):
    rows = pair[...].astype(F32)
    steps = [rows[:, i].reshape(FOLD * SIDE, WIDTH).T for i in range(STEPS)]
    return jnp.concatenate(steps, axis=1)


def columns_of(refs):
    rows = jnp.concatenate([ref[...] for ref in refs], axis=0)
    rest = jnp.zeros((WIDTH - rows.shape[0], WIDTH), F32)
    return jnp.concatenate([rows, rest], axis=0).T


def factors_of(proj):
    h = WIDTH
    left = times_sigmoid_of_double(proj[:h], proj[h : 2 * h])
    right = times_sigmoid_of_double(proj[2 * h : 3 * h], proj[3 * h : 4 * h])
    return left, right


def put_factors(scratch, left, right, factors):
    for step in range(STEPS):
        lanes = slice(step * 128, (step + 1) * 128)
        scratch[pl.ds(step, WIDTH, stride=2 * STEPS), :] = left[:, lanes]
        scratch[pl.ds(step + STEPS, WIDTH, stride=2 * STEPS), :] = right[:, lanes]
    rows = scratch[: WIDTH * 2 * STEPS]
    factors[...] = rows.reshape(WIDTH, 2 * STEPS, 128).astype(BF16)


def first_kernel(pair, norm_gain, norm_bias, weight, factors, scratch):
    vectors = columns_of((norm_gain, norm_bias))
    normed = layer_norm(field_of(pair), vectors[:, 0:1], vectors[:, 3:4]).astype(BF16)
    put_factors(scratch, *factors_of(dot(halved(weight[: 4 * WIDTH]), normed)), factors)


def middle_kernel(
    mixed, gates, fields, vectors, mixing, weight, out_weight, factors, fields_out, scratch, product
):
    gain, bias = vectors[:, 1:2], vectors[:, 4:5]
    mix_gain, mix_bias = mixing[:, 0:1], mixing[:, 2:3]
    field = finish(
        fields[...], take_mixed(mixed, product), mix_gain, mix_bias, out_weight[0].T, gates[...]
    )
    normed = layer_norm(field, gain, bias).astype(BF16)
    put_factors(scratch, *factors_of(dot(halved(weight[1, :, : 4 * WIDTH]).T, normed)), factors)
    fields_out[...] = field


def last_kernel(mixed, gates, fields, vectors, mixing, out_weight, up, down, updated, product):
    gain, bias = vectors[:, 2:3], vectors[:, 5:6]
    mix_gain, mix_bias = mixing[:, 1:2], mixing[:, 3:4]
    inner = down.shape[0]
    field = finish(
        fields[...], take_mixed(mixed, product), mix_gain, mix_bias, out_weight[1].T, gates[...]
    )
    tnorm = layer_norm(field, gain, bias).astype(BF16)
    half = dot(halved(up[:, :inner]).T, tnorm)
    act = (times_sigmoid_of_double(half, half) * dot(up[:, inner:].T, tnorm)).astype(BF16)
    field = field + dot(down[...].T, act)
    for i in range(STEPS):
        block = field[:, i * 128 : (i + 1) * 128].T.reshape(FOLD, SIDE, WIDTH)
        updated[:, i] = block.astype(BF16)


def turn(tiles):
    lane = lax.broadcasted_iota(jnp.int32, tiles[0].shape, 1)
    low = lane < 64
    even = (lane & 32) == 0

    def far(a, b):
        moved = pltpu.roll(jnp.where(low, b, a), 64, 1)
        return jnp.where(low, a, moved), jnp.where(low, moved, b)

    def near(a, b):
        return (
            jnp.where(even, a, pltpu.roll(b, 32, 1)),
            jnp.where(even, pltpu.roll(a, 96, 1), b),
        )

    a, b, c, d = tiles
    a, c = far(a, c)
    b, d = far(b, d)
    return *near(a, b), *near(c, d)


def lanes_from(g):
    return slice(g * 128, (g + 1) * 128)


def rows_of(source, columns, half):
    rows = slice(half * STEPS, (half + 1) * STEPS)
    tiles = [source[pl.ds(member(0, q), PAIRS)].astype(F32)[:, rows] for q in columns]
    tiles = turn([tile.reshape(PAIRS * STEPS, 128) for tile in tiles])
    tiles = [tile.reshape(PAIRS, 1, STEPS, 128) for tile in tiles]
    return jnp.concatenate(tiles, axis=1)


def flat_rows(block):
    return block.reshape(HALF, 128).astype(BF16)


def send_product(mixed, product, columns):
    mixed = mixed.reshape(PAIRS, FOLD, STEPS, SIDE * len(columns))
    for g in range(len(columns) // FOLD):
        tiles = [mixed[:, i, :, lanes_from(g)].reshape(PAIRS * STEPS, 128) for i in range(FOLD)]
        for i, tile in enumerate(turn(tiles)):
            rows = pl.ds(member(0, columns[g * FOLD + i]), PAIRS)
            product[rows] = tile.reshape(PAIRS, STEPS, 128).astype(BF16)


def dot_rows(left, right):
    return lax.dot_general(
        left[...], right[...], (((1,), (1,)), ((), ())), preferred_element_type=F32
    )


def dot_columns(left, right):
    return lax.dot_general(
        left[...], right[...], (((0,), (0,)), ((), ())), preferred_element_type=F32
    )


def outgoing_own_kernel(
    own, pair, norm_gain, norm_bias, weight,
    left, own_product, gates, fields, vectors, right,
):
    for g in range(COLS // FOLD):
        columns = [g * FOLD + i for i in range(FOLD)]
        left[:, lanes_from(g)] = flat_rows(rows_of(own, columns, 0))
        right[:, lanes_from(g)] = flat_rows(rows_of(own, columns, 1))
    send_product(dot_rows(left, right), own_product, range(PAIRS))
    vectors[...] = columns_of((norm_gain, norm_bias))
    field = field_of(pair)
    normed = layer_norm(field, vectors[:, 0:1], vectors[:, 3:4]).astype(BF16)
    gates[...] = sigmoid_of_double(dot(halved(weight[4 * WIDTH :]), normed))
    fields[...] = field


def outgoing_kernel(other, left, own_product, out_gain, out_bias, product, mixing, right):
    mixing[...] = columns_of((out_gain, out_bias))
    core = core_index()
    for g in range(COLS // FOLD):
        columns = [g * FOLD + i for i in range(FOLD)]
        right[:, lanes_from(g)] = flat_rows(rows_of(other, columns, 0))
    for a in range(PAIRS):
        rows = pl.ds(member(0, 2 * a + core), PAIRS)
        product[rows] = own_product[member(0, a) : member(0, a + 1)]
    send_product(dot_rows(left, right), product, [2 * a + 1 - core for a in range(PAIRS)])


def form_incoming(source, left, right):
    core = core_index()
    for g in range(COLS // FOLD):
        columns = [g * FOLD + i for i in range(FOLD)]
        right[:, lanes_from(g)] = flat_rows(rows_of(source, columns, 1))
    for g in range(PAIRS // FOLD):
        columns = [2 * (g * FOLD + i) + core for i in range(FOLD)]
        left[:, lanes_from(g)] = flat_rows(rows_of(source, columns, 0))


def incoming_own_kernel(own, fields, vectors, weight, own_mixed, gates, left, right):
    form_incoming(own, left, right)
    own_mixed[...] = dot_columns(left, right)
    normed = layer_norm(fields[...], vectors[:, 1:2], vectors[:, 4:5]).astype(BF16)
    gates[...] = sigmoid_of_double(dot(halved(weight[1, :, 4 * WIDTH :]).T, normed))


def incoming_kernel(other, own_mixed, product, left, right):
    form_incoming(other, left, right)
    send_product(own_mixed[...] + dot_columns(left, right), product, range(COLS))


def call(kernel, outs, scratch, name, vmem=40, **more):
    return pl.pallas_call(
        kernel,
        out_shape=outs,
        scratch_shapes=scratch,
        compiler_params=pltpu.CompilerParams(vmem_limit_bytes=int(vmem * 1024 * 1024)),
        name=name,
        **more,
    )


def shape(*dims, dtype=BF16):
    return jax.ShapeDtypeStruct(dims, dtype)


def body(
    pair, norm_gain, norm_bias, proj_weight, out_gain, out_bias, out_weight, up_weight, down_weight
):
    flat = shape(WIDTH, STEPS * 128, dtype=F32)
    packed = shape(WIDTH, 2 * STEPS, 128)
    product = shape(WIDTH, STEPS, 128)
    packing = pltpu.VMEM(((WIDTH + 1) * 2 * STEPS, 128), F32)
    unpacking = pltpu.VMEM(((WIDTH + 1) * STEPS, 128), F32)
    blocks = (FOLD, STEPS, SIDE, WIDTH)

    pair = pair.reshape(blocks)
    first_weight = proj_weight[0].T
    factors = call(first_kernel, packed, [packing], "first")(
        pair, norm_gain, norm_bias, first_weight
    )
    own = exchange(factors)
    other = swap_cores(own[:, STEPS:])
    wide, square = (HALF, FULL), (HALF, HALF)
    outs = (shape(*wide), shape(WIDTH // 2, STEPS, 128), flat, flat)
    factor, square = pltpu.VMEM(wide, BF16), pltpu.VMEM(square, BF16)
    left, own_product, gate, field, vectors = call(
        outgoing_own_kernel, (*outs, shape(WIDTH, WIDTH, dtype=F32)), [factor], "outgoing_own"
    )(own, pair, norm_gain, norm_bias, first_weight)
    square_f32 = shape(WIDTH, WIDTH, dtype=F32)
    mixed, mixing = call(outgoing_kernel, (product, square_f32), [factor], "outgoing")(
        other, left, own_product, out_gain, out_bias
    )
    factors, field = call(middle_kernel, (packed, flat), [packing, unpacking], "middle")(
        exchange(mixed), gate, field, vectors, mixing, proj_weight, out_weight
    )
    own = exchange(factors)
    other = swap_cores(own)
    outs = (shape(*wide, dtype=F32), flat)
    own_mixed, gate = call(incoming_own_kernel, outs, [square, factor], "incoming_own")(
        own, field, vectors, proj_weight
    )
    mixed = call(incoming_kernel, product, [square, factor], "incoming")(other, own_mixed)
    updated = call(last_kernel, shape(*blocks), [unpacking], "last")(
        exchange(mixed), gate, field, vectors, mixing, out_weight, up_weight, down_weight
    )
    return updated.reshape(FOLD * STEPS, SIDE, WIDTH)


def solution(mesh):
    placed = (P("row", "col", None), P(), P(), P(), P(), P(), P(), P(), P())
    return jax.shard_map(
        body, mesh=mesh, in_specs=placed, out_specs=P("row", "col", None), check_vma=False
    )
```
